512 devices in a mesh: row: 16 (over y, core), col: 32 (over x, z).
Axes of the slice: x: 4, y: 8, z: 8, core: 2. Of those that a mesh axis runs over, the one named last changes fastest.
Arguments:
- tokens: bfloat16 [2304, 8192], P('col', 'row'), may hold values from -6 to 6
- out_grad: bfloat16 [2304, 8192], P('col', 'row'), may hold values from -6 to 6
- gate_pre: bfloat16 [2304, 12288], P('row', 'col'), may hold values from -8 to 8
- up_pre: bfloat16 [2304, 12288], P('row', 'col'), may hold values from -6 to 6
- w_gate: bfloat16 [8192, 12288], P('row', 'col'), may hold values from -0.0625 to 0.0625
- w_up: bfloat16 [8192, 12288], P('row', 'col'), may hold values from -0.0625 to 0.0625
- w_down: bfloat16 [12288, 8192], P('col', 'row'), may hold values from -0.0546875 to 0.0546875
Outputs:
- token_grad: bfloat16 [2304, 8192], P('col', 'row')
- gate_wgrad: bfloat16 [8192, 12288], P('row', 'col')
- up_wgrad: bfloat16 [8192, 12288], P('row', 'col')
- down_wgrad: bfloat16 [12288, 8192], P('col', 'row')
The draws below stay inside these ranges and needn't reach their ends.
All inputs are finite; a program needn't handle non-finite values.
Results may differ from the reference program's by a relative error of at most 0.035.
Values may be sent and summed in bfloat16 or wider, within the bound.
No kernel may reach another device: no remote copies, remote signals or barrier semaphores. Data moves between devices by JAX's collectives and lax.ppermute only.
A program may use at most 64 MiB of HBM per device.

```python
import jax
import jax.numpy as jnp
from jax import lax

D = 8192
FF = 12288
TOKENS = 2304
N_ROW = 16
N_COL = 32


def steps_of(rng, extent, pieces, low, high):
    gain = 1.0
    for position, shards_of in pieces:
        draws = jax.random.uniform(jax.random.fold_in(jax.random.fold_in(rng, 6), position), (shards_of,), jnp.float32, low / len(pieces), high / len(pieces))
        gain = gain * jnp.repeat(jnp.exp(draws), extent[position] // shards_of).reshape((-1,) + (1,) * (len(extent) - 1 - position))
    return gain


def gaussian(stream_key, dims, width, limit, shards=(), kind=jnp.bfloat16):
    drawn = jax.random.normal(stream_key, dims, jnp.float32) * width
    if len(shards) > 0:
        drawn = steps_of(stream_key, dims, shards, -0.22, 0.18) * drawn
    return jnp.clip(drawn, min=-limit, max=limit).astype(kind)


def setup_inputs(seed: int = 0) -> dict:
    seeds = jax.random.split(jax.random.key(seed), 8)
    tokens = gaussian(seeds[0], (TOKENS, D), 1.0, 6.0, ((0, 32), (1, 16)))
    out_grad = gaussian(seeds[1], (TOKENS, D), 1.0, 6.0, ((0, 32), (1, 16)))
    gate_pre = gaussian(seeds[2], (TOKENS, FF), 1.5, 8.0, ((0, 16), (1, 32)))
    up_pre = gaussian(seeds[3], (TOKENS, FF), 1.0, 6.0, ((0, 16), (1, 32)))
    w_gate = gaussian(seeds[4], (D, FF), D ** -0.5, 0.0625, ((0, 16), (1, 32)))
    w_up = gaussian(seeds[5], (D, FF), D ** -0.5, 0.0625, ((0, 16), (1, 32)))
    w_down = gaussian(seeds[6], (FF, D), FF ** -0.5, 0.0546875, ((0, 32), (1, 16)))
    return dict(tokens=tokens, out_grad=out_grad, gate_pre=gate_pre, up_pre=up_pre, w_gate=w_gate, w_up=w_up, w_down=w_down)


def contract_last(left_side, right_side):
    return lax.dot_general(left_side, right_side, (((1,), (1,)), ((), ())), preferred_element_type=jnp.float32)


def contract_first(left_side, right_side):
    return lax.dot_general(left_side, right_side, (((0,), (0,)), ((), ())), preferred_element_type=jnp.float32)


def swiglu_grads(hidden_grad, gate_pre, up_pre):
    gate_float = gate_pre.astype(jnp.float32)
    up_float = up_pre.astype(jnp.float32)
    sigmoid_gate = jax.nn.sigmoid(gate_float)
    swish_gate = gate_float * sigmoid_gate
    gate_grad = (hidden_grad * up_float * sigmoid_gate * (1.0 + gate_float * (1.0 - sigmoid_gate))).astype(jnp.bfloat16)
    up_grad = (hidden_grad * swish_gate).astype(jnp.bfloat16)
    hidden = (swish_gate * up_float).astype(jnp.bfloat16)
    return gate_grad, up_grad, hidden


def reference(tokens, out_grad, gate_pre, up_pre, w_gate, w_up, w_down):
    feature_block = D // N_ROW

    def down_block(total, block_index):
        first_col = block_index * feature_block
        grad_piece = lax.dynamic_slice_in_dim(out_grad, first_col, feature_block, 1)
        weight_piece = lax.dynamic_slice_in_dim(w_down, first_col, feature_block, 1)
        block_term = lax.optimization_barrier(contract_last(grad_piece, weight_piece).astype(jnp.bfloat16))
        return total + block_term.astype(jnp.float32), None

    hidden_grad, leftover = lax.scan(down_block, jnp.zeros((TOKENS, FF), jnp.float32), jnp.arange(N_ROW, dtype=jnp.int32))
    gate_grad, up_grad, hidden = swiglu_grads(hidden_grad, gate_pre, up_pre)
    unit_block = FF // N_COL

    def input_block(total, block_index):
        first_col = block_index * unit_block
        gate_piece = lax.dynamic_slice_in_dim(gate_grad, first_col, unit_block, 1)
        up_piece = lax.dynamic_slice_in_dim(up_grad, first_col, unit_block, 1)
        gate_weight = lax.dynamic_slice_in_dim(w_gate, first_col, unit_block, 1)
        up_weight = lax.dynamic_slice_in_dim(w_up, first_col, unit_block, 1)
        block_term = contract_last(gate_piece, gate_weight) + contract_last(up_piece, up_weight)
        block_term = lax.optimization_barrier(block_term.astype(jnp.bfloat16))
        return total + block_term.astype(jnp.float32), None

    input_total, leftover_two = lax.scan(input_block, jnp.zeros((TOKENS, D), jnp.float32), jnp.arange(N_COL, dtype=jnp.int32))
    token_grad = input_total.astype(jnp.bfloat16)
    grad_scale = TOKENS ** -0.5
    gate_wgrad = (contract_first(tokens, gate_grad) * grad_scale).astype(jnp.bfloat16)
    up_wgrad = (contract_first(tokens, up_grad) * grad_scale).astype(jnp.bfloat16)
    down_wgrad = (contract_first(hidden, out_grad) * grad_scale).astype(jnp.bfloat16)
    return (token_grad, gate_wgrad, up_wgrad, down_wgrad)
```

```python
import jax
import jax.numpy as jnp
from jax import lax
from jax.sharding import PartitionSpec as P

N_CORE = 2
N_Z = 8


def contract_last(left_side, right_side):
    return lax.dot_general(
        left_side, right_side, (((1,), (1,)), ((), ())), preferred_element_type=jnp.float32
    )


def contract_first(left_side, right_side):
    return lax.dot_general(
        left_side, right_side, (((0,), (0,)), ((), ())), preferred_element_type=jnp.float32
    )


def swiglu_grads(hidden_grad, gate_pre, up_pre):
    gate_float = gate_pre.astype(jnp.float32)
    up_float = up_pre.astype(jnp.float32)
    sigmoid_gate = jax.nn.sigmoid(gate_float)
    swish_gate = gate_float * sigmoid_gate
    gate_grad = (
        hidden_grad * up_float * sigmoid_gate * (1.0 + gate_float * (1.0 - sigmoid_gate))
    ).astype(jnp.bfloat16)
    up_grad = (hidden_grad * swish_gate).astype(jnp.bfloat16)
    hidden = (swish_gate * up_float).astype(jnp.bfloat16)
    return (gate_grad, up_grad, hidden)


def exchange(pieces, axis, groups):
    return lax.all_to_all(pieces, axis, 0, 0, tiled=True, axis_index_groups=groups)


def spread(block, size, axis, groups):
    return exchange(jnp.broadcast_to(block[None], (size,) + block.shape), axis, groups)


def local(n_row, n_col, tokens, out_grad, gate_pre, up_pre, w_gate, w_up, w_down):
    n_y, n_x = n_row // N_CORE, n_col // N_Z
    z_groups = [[x * N_Z + z for z in range(N_Z)] for x in range(n_x)]
    x_groups = [[x * N_Z + z for x in range(n_x)] for z in range(N_Z)]
    y_groups = [[y * N_CORE + c for y in range(n_y)] for c in range(N_CORE)]
    core_swap = [(r, r ^ 1) for r in range(n_row)]
    core = lax.rem(lax.axis_index("row"), N_CORE)
    x_here = lax.div(lax.axis_index("col"), N_Z)
    units = gate_pre.shape[1]
    features = tokens.shape[1]
    rows = gate_pre.shape[0]

    saved = lax.all_gather(
        jnp.concatenate([gate_pre, up_pre], axis=1), "row", axis=0, tiled=True
    )
    total_rows = saved.shape[0]
    grad_z = spread(out_grad, N_Z, "col", z_groups)
    grad_rows = spread(
        grad_z.reshape(-1, features), n_x, "col", x_groups
    ).reshape(total_rows, features)

    part = contract_last(grad_rows, w_down).astype(jnp.bfloat16)
    part = part.reshape(n_y, N_CORE, rows, units)
    keep = lax.dynamic_index_in_dim(part, core, 1, keepdims=False)
    give = lax.dynamic_index_in_dim(part, 1 - core, 1, keepdims=False)
    got = lax.ppermute(give, "row", core_swap)
    pair = (keep.astype(jnp.float32) + got.astype(jnp.float32)).astype(jnp.bfloat16)
    terms = exchange(pair, "row", y_groups)
    share = jnp.sum(terms.astype(jnp.float32), axis=0).astype(jnp.bfloat16)

    own = spread(share, n_y, "row", y_groups)
    tokens, saved = lax.optimization_barrier((tokens, saved))
    token_rows = lax.all_gather(tokens, "col", axis=0, tiled=True)
    other = lax.ppermute(own, "row", core_swap)
    hidden_grad = jnp.where(
        core == 0, jnp.stack([own, other], axis=1), jnp.stack([other, own], axis=1)
    ).reshape(total_rows, units)
    gate_grad, up_grad, hidden = swiglu_grads(
        hidden_grad.astype(jnp.float32), saved[:, :units], saved[:, units:]
    )
    part_in = (contract_last(gate_grad, w_gate) + contract_last(up_grad, w_up)).astype(
        jnp.bfloat16
    )
    part_in = part_in.reshape(n_x, -1, features)
    total = lax.dynamic_index_in_dim(part_in, x_here, 0, keepdims=False).astype(jnp.float32)
    for step in range(1, n_x):
        moves = [
            (x * N_Z + z, (x + step) % n_x * N_Z + z) for x in range(n_x) for z in range(N_Z)
        ]
        piece = lax.dynamic_index_in_dim(
            part_in, lax.rem(x_here + step, n_x), 0, keepdims=False
        )
        total = total + lax.ppermute(piece, "col", moves).astype(jnp.float32)
    total = total.astype(jnp.bfloat16).reshape(N_Z, -1, features)
    token_terms = exchange(total, "col", z_groups)
    token_grad = jnp.sum(token_terms.astype(jnp.float32), axis=0).astype(jnp.bfloat16)

    grad_scale = total_rows ** (-0.5)
    gate_wgrad = (contract_first(token_rows, gate_grad) * grad_scale).astype(jnp.bfloat16)
    up_wgrad = (contract_first(token_rows, up_grad) * grad_scale).astype(jnp.bfloat16)
    down_wgrad = (contract_first(hidden, grad_rows) * grad_scale).astype(jnp.bfloat16)
    return (token_grad, gate_wgrad, up_wgrad, down_wgrad)


def solution(mesh):
    n_row, n_col = mesh.shape["row"], mesh.shape["col"]

    def device_program(*arrays):
        return local(n_row, n_col, *arrays)

    return jax.shard_map(
        device_program,
        mesh=mesh,
        in_specs=(
            P("col", "row"),
            P("col", "row"),
            P("row", "col"),
            P("row", "col"),
            P("row", "col"),
            P("row", "col"),
            P("col", "row"),
        ),
        out_specs=(P("col", "row"), P("row", "col"), P("row", "col"), P("col", "row")),
        check_vma=False,
    )
```

```python
import jax
import jax.numpy as jnp
from jax import lax
from jax.sharding import PartitionSpec as P

N_CORE = 2
N_Z = 8


def contract_last(left_side, right_side):
    return lax.dot_general(
        left_side, right_side, (((1,), (1,)), ((), ())), preferred_element_type=jnp.float32
    )


def contract_first(left_side, right_side):
    return lax.dot_general(
        left_side, right_side, (((0,), (0,)), ((), ())), preferred_element_type=jnp.float32
    )


def swiglu_grads(hidden_grad, gate_pre, up_pre):
    gate_float = gate_pre.astype(jnp.float32)
    up_float = up_pre.astype(jnp.float32)
    sigmoid_gate = jax.nn.sigmoid(gate_float)
    swish_gate = gate_float * sigmoid_gate
    gate_grad = (
        hidden_grad * up_float * sigmoid_gate * (1.0 + gate_float * (1.0 - sigmoid_gate))
    ).astype(jnp.bfloat16)
    up_grad = (hidden_grad * swish_gate).astype(jnp.bfloat16)
    hidden = (swish_gate * up_float).astype(jnp.bfloat16)
    return (gate_grad, up_grad, hidden)


def exchange(pieces, axis, groups):
    return lax.all_to_all(pieces, axis, 0, 0, tiled=True, axis_index_groups=groups)


def spread(block, size, axis, groups):
    return exchange(jnp.broadcast_to(block[None], (size,) + block.shape), axis, groups)


def local(n_row, n_col, tokens, out_grad, gate_pre, up_pre, w_gate, w_up, w_down):
    n_y, n_x = n_row // N_CORE, n_col // N_Z
    z_groups = [[x * N_Z + z for z in range(N_Z)] for x in range(n_x)]
    x_groups = [[x * N_Z + z for x in range(n_x)] for z in range(N_Z)]
    y_groups = [[y * N_CORE + c for y in range(n_y)] for c in range(N_CORE)]
    core_swap = [(r, r ^ 1) for r in range(n_row)]
    core = lax.rem(lax.axis_index("row"), N_CORE)
    x_here = lax.div(lax.axis_index("col"), N_Z)
    units = gate_pre.shape[1]
    features = tokens.shape[1]
    rows = gate_pre.shape[0]

    saved = lax.all_gather(
        jnp.concatenate([gate_pre, up_pre], axis=1), "row", axis=0, tiled=True
    )
    total_rows = saved.shape[0]
    grad_z = spread(out_grad, N_Z, "col", z_groups)
    grad_rows = spread(
        grad_z.reshape(-1, features), n_x, "col", x_groups
    ).reshape(total_rows, features)

    part = contract_last(grad_rows, w_down).astype(jnp.bfloat16)
    part = part.reshape(n_y, N_CORE, rows, units)
    keep = lax.dynamic_index_in_dim(part, core, 1, keepdims=False)
    give = lax.dynamic_index_in_dim(part, 1 - core, 1, keepdims=False)
    got = lax.ppermute(give, "row", core_swap)
    pair = (keep.astype(jnp.float32) + got.astype(jnp.float32)).astype(jnp.bfloat16)
    terms = exchange(pair, "row", y_groups)
    share = jnp.sum(terms.astype(jnp.float32), axis=0).astype(jnp.bfloat16)

    own = spread(share, n_y, "row", y_groups)
    token_rows = lax.all_gather(tokens, "col", axis=0, tiled=True)
    other = lax.ppermute(own, "row", core_swap)
    hidden_grad = jnp.where(
        core == 0, jnp.stack([own, other], axis=1), jnp.stack([other, own], axis=1)
    ).reshape(total_rows, units)
    gate_grad, up_grad, hidden = swiglu_grads(
        hidden_grad.astype(jnp.float32), saved[:, :units], saved[:, units:]
    )
    part_in = (contract_last(gate_grad, w_gate) + contract_last(up_grad, w_up)).astype(
        jnp.bfloat16
    )
    part_in = part_in.reshape(n_x, -1, features)
    total = lax.dynamic_index_in_dim(part_in, x_here, 0, keepdims=False).astype(jnp.float32)
    for step in range(1, n_x):
        moves = [
            (x * N_Z + z, (x + step) % n_x * N_Z + z) for x in range(n_x) for z in range(N_Z)
        ]
        piece = lax.dynamic_index_in_dim(
            part_in, lax.rem(x_here + step, n_x), 0, keepdims=False
        )
        total = total + lax.ppermute(piece, "col", moves).astype(jnp.float32)
    total = total.astype(jnp.bfloat16).reshape(N_Z, -1, features)
    token_terms = exchange(total, "col", z_groups)
    token_grad = jnp.sum(token_terms.astype(jnp.float32), axis=0).astype(jnp.bfloat16)

    grad_scale = total_rows ** (-0.5)
    gate_wgrad = (contract_first(token_rows, gate_grad) * grad_scale).astype(jnp.bfloat16)
    up_wgrad = (contract_first(token_rows, up_grad) * grad_scale).astype(jnp.bfloat16)
    down_wgrad = (contract_first(hidden, grad_rows) * grad_scale).astype(jnp.bfloat16)
    return (token_grad, gate_wgrad, up_wgrad, down_wgrad)


def solution(mesh):
    n_row, n_col = mesh.shape["row"], mesh.shape["col"]

    def device_program(*arrays):
        return local(n_row, n_col, *arrays)

    return jax.shard_map(
        device_program,
        mesh=mesh,
        in_specs=(
            P("col", "row"),
            P("col", "row"),
            P("row", "col"),
            P("row", "col"),
            P("row", "col"),
            P("row", "col"),
            P("col", "row"),
        ),
        out_specs=(P("col", "row"), P("row", "col"), P("row", "col"), P("col", "row")),
        check_vma=False,
    )
```

```python
import jax
import jax.numpy as jnp
from jax import lax
from jax.sharding import PartitionSpec as P

N_CORE = 2
N_Z = 8


def contract_last(left_side, right_side):
    return lax.dot_general(
        left_side, right_side, (((1,), (1,)), ((), ())), preferred_element_type=jnp.float32
    )


def contract_first(left_side, right_side):
    return lax.dot_general(
        left_side, right_side, (((0,), (0,)), ((), ())), preferred_element_type=jnp.float32
    )


def swiglu_inputs(hidden_grad, gate_pre, up_pre):
    gate_float = gate_pre.astype(jnp.float32)
    up_float = up_pre.astype(jnp.float32)
    grad_float = hidden_grad.astype(jnp.float32)
    sigmoid_gate = jax.nn.sigmoid(gate_float)
    swish_gate = gate_float * sigmoid_gate
    gate_grad = (
        grad_float * up_float * sigmoid_gate * (1.0 + gate_float * (1.0 - sigmoid_gate))
    ).astype(jnp.bfloat16)
    up_grad = (grad_float * swish_gate).astype(jnp.bfloat16)
    hidden = (swish_gate * up_float).astype(jnp.bfloat16)
    return (gate_grad, up_grad, hidden)


def exchange(pieces, axis, groups):
    return lax.all_to_all(pieces, axis, 0, 0, tiled=True, axis_index_groups=groups)


def spread(block, size, axis, groups):
    return exchange(jnp.broadcast_to(block[None], (size,) + block.shape), axis, groups)


def pick(stacked, index, axis=0):
    return lax.dynamic_index_in_dim(stacked, index, axis, keepdims=False)


def local(n_row, n_col, tokens, out_grad, gate_pre, up_pre, w_gate, w_up, w_down):
    n_y, n_x = n_row // N_CORE, n_col // N_Z
    z_groups = [[x * N_Z + z for z in range(N_Z)] for x in range(n_x)]
    x_groups = [[x * N_Z + z for x in range(n_x)] for z in range(N_Z)]
    y_groups = [[y * N_CORE + c for y in range(n_y)] for c in range(N_CORE)]
    core_swap = [(r, r ^ 1) for r in range(n_row)]
    row_here, col_here = lax.axis_index("row"), lax.axis_index("col")
    core, y_here = lax.rem(row_here, N_CORE), lax.div(row_here, N_CORE)
    x_here = lax.div(col_here, N_Z)
    rows, units = gate_pre.shape
    block, features = out_grad.shape
    half = 2 * units
    group_rows = N_Z * block

    def x_shift(step):
        return [
            (x * N_Z + z, (x + step) % n_x * N_Z + z) for x in range(n_x) for z in range(N_Z)
        ]

    def to_group(turn):
        pairs = []
        for r in range(n_row):
            for x in range(n_x):
                piece = (turn + x) % 2
                new_row = (2 * (r % n_x) + piece) * N_CORE + x // 2
                for z in range(N_Z):
                    pairs.append((r * n_col + x * N_Z + z, new_row * n_col + r // n_x * N_Z + z))
        return pairs

    def to_shard(turn):
        pairs = []
        for y in range(n_y):
            for c in range(N_CORE):
                slot = (turn + y) % 2
                for x in range(n_x):
                    for z in range(N_Z):
                        source = (y * N_CORE + c) * n_col + x * N_Z + z
                        new_row = n_x * x + y // 2
                        pairs.append((source, new_row * n_col + (2 * c + slot) * N_Z + z))
        return pairs

    down_all = lax.all_gather(
        w_down, "col", axis=0, tiled=True, axis_index_groups=x_groups
    ).reshape(N_CORE, half, features)

    saved_pieces = jnp.concatenate([gate_pre, up_pre], axis=1).reshape(2, block, half)
    moved = [
        lax.ppermute(
            pick(saved_pieces, lax.rem(x_here + turn, 2)), ("row", "col"), to_group(turn)
        )
        for turn in range(2)
    ]
    y_even = lax.rem(y_here, 2) == 0
    first = jnp.where(y_even, moved[0], moved[1])
    second = jnp.where(y_even, moved[1], moved[0])
    saved_share = jnp.concatenate(
        [first[:, :units], second[:, :units], first[:, units:], second[:, units:]], axis=1
    )
    saved = lax.all_gather(saved_share, "row", axis=0, tiled=True).reshape(
        n_y, N_CORE, block, 2 * half
    )

    both = spread(jnp.concatenate([out_grad, tokens], axis=1), N_Z, "col", z_groups).reshape(
        group_rows, 2 * features
    )
    grad_rows = both[:, :features]

    w_both = jnp.concatenate([w_gate, w_up], axis=1)
    w_stack = jnp.stack(
        [w_both] + [lax.ppermute(w_both, "col", x_shift(step)) for step in range(1, n_x)]
    )
    w_order = [
        pick(w_stack, lax.rem(x_here - 2 * core - place + 2 * n_x, n_x)) for place in range(n_x)
    ]

    def w_half(side, which):
        pieces = w_order[2 * side : 2 * side + 2]
        return jnp.concatenate(
            [piece[:, which * units : (which + 1) * units] for piece in pieces], axis=1
        )

    give = contract_last(grad_rows, pick(down_all, 1 - core)).astype(jnp.bfloat16)
    got = lax.ppermute(give, "row", core_swap)
    keep = contract_last(grad_rows, pick(down_all, core)).astype(jnp.bfloat16)
    pair = (keep.astype(jnp.float32) + got.astype(jnp.float32)).astype(jnp.bfloat16)
    terms = exchange(pair.reshape(n_y, block, half), "row", y_groups)
    share = jnp.sum(terms.astype(jnp.float32), axis=0).astype(jnp.bfloat16)

    sent = [
        lax.ppermute(
            jnp.where(lax.rem(y_here + turn, 2) == 0, share[:, :units], share[:, units:]),
            ("row", "col"),
            to_shard(turn),
        )
        for turn in range(2)
    ]
    x_even = lax.rem(x_here, 2) == 0
    shard_grad = jnp.concatenate(
        [jnp.where(x_even, sent[0], sent[1]), jnp.where(x_even, sent[1], sent[0])], axis=0
    )
    unit_arrays = lax.all_gather(
        jnp.concatenate(swiglu_inputs(shard_grad, gate_pre, up_pre), axis=1),
        "row",
        axis=0,
        tiled=True,
    )
    total_rows = unit_arrays.shape[0]

    own = spread(share, n_y, "row", y_groups)
    other = lax.ppermute(own, "row", core_swap)
    part_in = 0.0
    for side, hidden_grad in enumerate((own, other)):
        side_saved = pick(saved, lax.rem(core + side, 2), 1)
        gate_grad, up_grad, _ = swiglu_inputs(
            hidden_grad, side_saved[..., :half], side_saved[..., half:]
        )
        part_in = part_in + contract_last(gate_grad.reshape(group_rows, half), w_half(side, 0))
        part_in = part_in + contract_last(up_grad.reshape(group_rows, half), w_half(side, 1))
    token_terms = exchange(
        part_in.astype(jnp.bfloat16).reshape(N_Z, block, features), "col", z_groups
    )
    token_grad = jnp.sum(token_terms.astype(jnp.float32), axis=0).astype(jnp.bfloat16)

    all_rows = jnp.zeros((n_x,) + both.shape, both.dtype)
    for step in range(n_x):
        piece = lax.ppermute(both, "col", x_shift(step)) if step else both
        all_rows = lax.dynamic_update_index_in_dim(
            all_rows, piece, lax.rem(x_here - step + n_x, n_x), 0
        )
    all_rows = all_rows.reshape(total_rows, 2 * features)
    grad_scale = total_rows ** (-0.5)
    gate_wgrad, up_wgrad = (
        (
            contract_first(all_rows[:, features:], unit_arrays[:, k * units : (k + 1) * units])
            * grad_scale
        ).astype(jnp.bfloat16)
        for k in range(2)
    )
    down_wgrad = (
        contract_first(unit_arrays[:, 2 * units :], all_rows[:, :features]) * grad_scale
    ).astype(jnp.bfloat16)
    return (token_grad, gate_wgrad, up_wgrad, down_wgrad)


def solution(mesh):
    n_row, n_col = mesh.shape["row"], mesh.shape["col"]

    def device_program(*arrays):
        return local(n_row, n_col, *arrays)

    return jax.shard_map(
        device_program,
        mesh=mesh,
        in_specs=(
            P("col", "row"),
            P("col", "row"),
            P("row", "col"),
            P("row", "col"),
            P("row", "col"),
            P("row", "col"),
            P("col", "row"),
        ),
        out_specs=(P("col", "row"), P("row", "col"), P("row", "col"), P("col", "row")),
        check_vma=False,
    )
```

```python
import jax
import jax.numpy as jnp
from jax import lax
from jax.sharding import PartitionSpec as P

N_CORE = 2
N_Z = 8


def contract_last(left_side, right_side):
    return lax.dot_general(
        left_side, right_side, (((1,), (1,)), ((), ())), preferred_element_type=jnp.float32
    )


def contract_first(left_side, right_side):
    return lax.dot_general(
        left_side, right_side, (((0,), (0,)), ((), ())), preferred_element_type=jnp.float32
    )


def swiglu_grads(hidden_grad, gate_pre, up_pre):
    gate_float = gate_pre.astype(jnp.float32)
    up_float = up_pre.astype(jnp.float32)
    grad_float = hidden_grad.astype(jnp.float32)
    sigmoid_gate = jax.nn.sigmoid(gate_float)
    gate_grad = grad_float * up_float * sigmoid_gate * (1.0 + gate_float * (1.0 - sigmoid_gate))
    up_grad = grad_float * (gate_float * sigmoid_gate)
    return gate_grad.astype(jnp.bfloat16), up_grad.astype(jnp.bfloat16)


def swiglu_hidden(gate_pre, up_pre):
    gate_float = gate_pre.astype(jnp.float32)
    swish_gate = gate_float * jax.nn.sigmoid(gate_float)
    return (swish_gate * up_pre.astype(jnp.float32)).astype(jnp.bfloat16)


def exchange(pieces, axis, groups):
    return lax.all_to_all(pieces, axis, 0, 0, tiled=True, axis_index_groups=groups)


def spread(block, size, axis, groups):
    return exchange(jnp.broadcast_to(block[None], (size,) + block.shape), axis, groups)


def pick(stacked, index, axis=0):
    return lax.dynamic_index_in_dim(stacked, index, axis, keepdims=False)


def local(n_row, n_col, tokens, out_grad, gate_pre, up_pre, w_gate, w_up, w_down):
    n_y, n_x = n_row // N_CORE, n_col // N_Z
    z_groups = [[x * N_Z + z for z in range(N_Z)] for x in range(n_x)]
    x_groups = [[x * N_Z + z for x in range(n_x)] for z in range(N_Z)]
    y_groups = [[y * N_CORE + c for y in range(n_y)] for c in range(N_CORE)]
    core_swap = [(r, r ^ 1) for r in range(n_row)]
    row_here, col_here = lax.axis_index("row"), lax.axis_index("col")
    core, y_here = lax.rem(row_here, N_CORE), lax.div(row_here, N_CORE)
    x_here = lax.div(col_here, N_Z)
    rows, units = gate_pre.shape
    block, features = out_grad.shape
    half = 2 * units
    group_rows = N_Z * block

    def x_shift(step):
        return [
            (x * N_Z + z, (x + step) % n_x * N_Z + z) for x in range(n_x) for z in range(N_Z)
        ]

    def to_group(turn):
        pairs = []
        for r in range(n_row):
            for x in range(n_x):
                piece = (turn + x) % 2
                new_row = (2 * (r % n_x) + piece) * N_CORE + x // 2
                for z in range(N_Z):
                    pairs.append((r * n_col + x * N_Z + z, new_row * n_col + r // n_x * N_Z + z))
        return pairs

    down_all = lax.all_gather(
        w_down, "col", axis=0, tiled=True, axis_index_groups=x_groups
    ).reshape(N_CORE, half, features)

    grad_rows = spread(out_grad, N_Z, "col", z_groups).reshape(group_rows, features)
    tokens, grad_rows = lax.optimization_barrier((tokens, grad_rows))
    token_rows = spread(tokens, N_Z, "col", z_groups).reshape(group_rows, features)

    saved_pieces = jnp.concatenate([gate_pre, up_pre], axis=1).reshape(2, block, half)
    moved = [
        lax.ppermute(
            pick(saved_pieces, lax.rem(x_here + turn, 2)), ("row", "col"), to_group(turn)
        )
        for turn in range(2)
    ]
    y_even = lax.rem(y_here, 2) == 0
    first = jnp.where(y_even, moved[0], moved[1])
    second = jnp.where(y_even, moved[1], moved[0])
    saved_share = jnp.concatenate(
        [first[:, :units], second[:, :units], first[:, units:], second[:, units:]], axis=1
    )
    saved = lax.all_gather(saved_share, "row", axis=0, tiled=True).reshape(
        n_y, N_CORE, block, 2 * half
    )

    w_both = jnp.concatenate([w_gate, w_up], axis=1)
    w_both, down_all = lax.optimization_barrier((w_both, down_all))
    w_left = lax.ppermute(w_both, "col", x_shift(1))
    w_right = lax.ppermute(w_both, "col", x_shift(n_x - 1))
    w_far = lax.ppermute(w_left, "col", x_shift(1))

    give = contract_last(grad_rows, pick(down_all, 1 - core)).astype(jnp.bfloat16)
    got = lax.ppermute(give, "row", core_swap)
    keep = contract_last(grad_rows, pick(down_all, core)).astype(jnp.bfloat16)
    pair = (keep.astype(jnp.float32) + got.astype(jnp.float32)).astype(jnp.bfloat16)
    pair, token_rows = lax.optimization_barrier((pair, token_rows))
    terms = exchange(pair.reshape(n_y, block, half), "row", y_groups)
    share = jnp.sum(terms.astype(jnp.float32), axis=0).astype(jnp.bfloat16)
    own = spread(share, n_y, "row", y_groups)

    grad_scale = (rows * n_row) ** (-0.5)

    def side_saved(side):
        return saved[:, side, :, :half], saved[:, side, :, half:]

    down_part = []
    for side in range(2):
        hidden = swiglu_hidden(*side_saved(side)).reshape(group_rows, half)
        down_part.append(contract_first(hidden, grad_rows).astype(jnp.bfloat16))
    down_part = jnp.concatenate(down_part, axis=0)
    own, _ = lax.optimization_barrier((own, down_part))
    down_sum = lax.psum_scatter(
        down_part,
        "col",
        scatter_dimension=0,
        tiled=True,
        axis_index_groups=x_groups,
    )
    down_wgrad = (down_sum.astype(jnp.float32) * grad_scale).astype(jnp.bfloat16)

    own, w_left, w_right, w_far = lax.optimization_barrier((own, w_left, w_right, w_far))
    w_stack = jnp.stack([w_both, w_left, w_far, w_right])
    w_order = [pick(w_stack, lax.rem(x_here - place + n_x, n_x)) for place in range(n_x)]

    def w_half(side, which):
        pieces = w_order[2 * side : 2 * side + 2]
        return jnp.concatenate(
            [piece[:, which * units : (which + 1) * units] for piece in pieces], axis=1
        )

    other = lax.ppermute(own, "row", core_swap)
    part_in, gate_part, up_part = 0.0, [], []
    for side in range(2):
        hidden_grad = jnp.where(core == side, own, other)
        gate_grad, up_grad = swiglu_grads(hidden_grad, *side_saved(side))
        gate_grad = gate_grad.reshape(group_rows, half)
        up_grad = up_grad.reshape(group_rows, half)
        part_in = part_in + contract_last(gate_grad, w_half(side, 0))
        part_in = part_in + contract_last(up_grad, w_half(side, 1))
        for slot in range(2):
            columns = slice(slot * units, (slot + 1) * units)
            gate_part.append(contract_first(token_rows, gate_grad[:, columns]))
            up_part.append(contract_first(token_rows, up_grad[:, columns]))
    unit_sum = lax.psum_scatter(
        jnp.stack(
            [jnp.concatenate(parts, axis=1) for parts in zip(gate_part, up_part)]
        ).astype(jnp.bfloat16),
        "col",
        scatter_dimension=0,
        tiled=True,
        axis_index_groups=x_groups,
    )[0]
    unit_wgrad = (unit_sum.astype(jnp.float32) * grad_scale).astype(jnp.bfloat16)
    gate_wgrad, up_wgrad = unit_wgrad[:, :units], unit_wgrad[:, units:]
    token_terms = exchange(
        part_in.astype(jnp.bfloat16).reshape(N_Z, block, features), "col", z_groups
    )
    token_grad = jnp.sum(token_terms.astype(jnp.float32), axis=0).astype(jnp.bfloat16)
    return (token_grad, gate_wgrad, up_wgrad, down_wgrad)


def solution(mesh):
    n_row, n_col = mesh.shape["row"], mesh.shape["col"]

    def device_program(*arrays):
        return local(n_row, n_col, *arrays)

    return jax.shard_map(
        device_program,
        mesh=mesh,
        in_specs=(
            P("col", "row"),
            P("col", "row"),
            P("row", "col"),
            P("row", "col"),
            P("row", "col"),
            P("row", "col"),
            P("col", "row"),
        ),
        out_specs=(P("col", "row"), P("row", "col"), P("row", "col"), P("col", "row")),
        check_vma=False,
    )
```

```python
import jax
import jax.numpy as jnp
from jax import lax
from jax.sharding import PartitionSpec as P

N_CORE = 2
N_Z = 8


def contract_last(left_side, right_side):
    return lax.dot_general(
        left_side, right_side, (((1,), (1,)), ((), ())), preferred_element_type=jnp.float32
    )


def contract_first(left_side, right_side):
    return lax.dot_general(
        left_side, right_side, (((0,), (0,)), ((), ())), preferred_element_type=jnp.float32
    )


def swiglu_grads(hidden_grad, gate_pre, up_pre):
    gate_float = gate_pre.astype(jnp.float32)
    up_float = up_pre.astype(jnp.float32)
    grad_float = hidden_grad.astype(jnp.float32)
    sigmoid_gate = jax.nn.sigmoid(gate_float)
    gate_grad = grad_float * up_float * sigmoid_gate * (1.0 + gate_float * (1.0 - sigmoid_gate))
    up_grad = grad_float * (gate_float * sigmoid_gate)
    return gate_grad.astype(jnp.bfloat16), up_grad.astype(jnp.bfloat16)


def swiglu_hidden(gate_pre, up_pre):
    gate_float = gate_pre.astype(jnp.float32)
    swish_gate = gate_float * jax.nn.sigmoid(gate_float)
    return (swish_gate * up_pre.astype(jnp.float32)).astype(jnp.bfloat16)


def exchange(pieces, axis, groups):
    return lax.all_to_all(pieces, axis, 0, 0, tiled=True, axis_index_groups=groups)


def spread(block, size, axis, groups):
    return exchange(jnp.broadcast_to(block[None], (size,) + block.shape), axis, groups)


def pick(stacked, index, axis=0):
    return lax.dynamic_index_in_dim(stacked, index, axis, keepdims=False)


def local(n_row, n_col, tokens, out_grad, gate_pre, up_pre, w_gate, w_up, w_down):
    n_y, n_x = n_row // N_CORE, n_col // N_Z
    z_groups = [[x * N_Z + z for z in range(N_Z)] for x in range(n_x)]
    x_groups = [[x * N_Z + z for x in range(n_x)] for z in range(N_Z)]
    y_groups = [[y * N_CORE + c for y in range(n_y)] for c in range(N_CORE)]
    core_swap = [(r, r ^ 1) for r in range(n_row)]
    row_here, col_here = lax.axis_index("row"), lax.axis_index("col")
    core, y_here = lax.rem(row_here, N_CORE), lax.div(row_here, N_CORE)
    x_here = lax.div(col_here, N_Z)
    rows, units = gate_pre.shape
    block, features = out_grad.shape
    half = 2 * units
    group_rows = N_Z * block

    def x_shift(step):
        return [
            (x * N_Z + z, (x + step) % n_x * N_Z + z) for x in range(n_x) for z in range(N_Z)
        ]

    def to_group(turn):
        pairs = []
        for r in range(n_row):
            for x in range(n_x):
                piece = (turn + x) % 2
                new_row = (2 * (r % n_x) + piece) * N_CORE + x // 2
                for z in range(N_Z):
                    pairs.append((r * n_col + x * N_Z + z, new_row * n_col + r // n_x * N_Z + z))
        return pairs

    down_all = lax.all_gather(
        w_down, "col", axis=0, tiled=True, axis_index_groups=x_groups
    ).reshape(N_CORE, half, features)

    grad_rows = spread(out_grad, N_Z, "col", z_groups).reshape(group_rows, features)

    saved_pieces = jnp.concatenate([gate_pre, up_pre], axis=1).reshape(2, block, half)
    moved = [
        lax.ppermute(
            pick(saved_pieces, lax.rem(x_here + turn, 2)), ("row", "col"), to_group(turn)
        )
        for turn in range(2)
    ]
    y_even = lax.rem(y_here, 2) == 0
    first = jnp.where(y_even, moved[0], moved[1])
    second = jnp.where(y_even, moved[1], moved[0])
    saved_share = jnp.concatenate(
        [first[:, :units], second[:, :units], first[:, units:], second[:, units:]], axis=1
    )
    saved = lax.all_gather(saved_share, "row", axis=0, tiled=True).reshape(
        n_y, N_CORE, block, 2 * half
    )

    both = jnp.concatenate([tokens, out_grad], axis=1)
    both, saved_share = lax.optimization_barrier((both, saved_share))
    token_rows = lax.all_gather(both, "col", axis=0, tiled=True, axis_index_groups=z_groups)[
        :, :features
    ]

    w_both = jnp.concatenate([w_gate, w_up], axis=1)
    w_both, down_all = lax.optimization_barrier((w_both, down_all))
    w_left = lax.ppermute(w_both, "col", x_shift(1))
    w_right = lax.ppermute(w_both, "col", x_shift(n_x - 1))
    w_far = lax.ppermute(w_left, "col", x_shift(1))

    give = contract_last(grad_rows, pick(down_all, 1 - core)).astype(jnp.bfloat16)
    got = lax.ppermute(give, "row", core_swap)
    keep = contract_last(grad_rows, pick(down_all, core)).astype(jnp.bfloat16)
    pair = (keep.astype(jnp.float32) + got.astype(jnp.float32)).astype(jnp.bfloat16)
    terms = exchange(pair.reshape(n_y, block, half), "row", y_groups)
    share = jnp.sum(terms.astype(jnp.float32), axis=0).astype(jnp.bfloat16)
    own = spread(share, n_y, "row", y_groups)

    grad_scale = (rows * n_row) ** (-0.5)

    def side_saved(side):
        return saved[:, side, :, :half], saved[:, side, :, half:]

    down_part = []
    for side in range(2):
        hidden = swiglu_hidden(*side_saved(side)).reshape(group_rows, half)
        down_part.append(contract_first(hidden, grad_rows).astype(jnp.bfloat16))
    down_part = jnp.concatenate(down_part, axis=0)
    own, _ = lax.optimization_barrier((own, down_part))
    down_sum = lax.psum_scatter(
        down_part,
        "col",
        scatter_dimension=0,
        tiled=True,
        axis_index_groups=x_groups,
    )

    own, w_left, w_right, w_far = lax.optimization_barrier((own, w_left, w_right, w_far))
    w_stack = jnp.stack([w_both, w_left, w_far, w_right])
    w_order = [pick(w_stack, lax.rem(x_here - place + n_x, n_x)) for place in range(n_x)]

    def w_half(side, which):
        pieces = w_order[2 * side : 2 * side + 2]
        return jnp.concatenate(
            [piece[:, which * units : (which + 1) * units] for piece in pieces], axis=1
        )

    other = lax.ppermute(own, "row", core_swap)
    part_in, gate_part, up_part = 0.0, [], []
    for side in range(2):
        hidden_grad = jnp.where(core == side, own, other)
        gate_grad, up_grad = swiglu_grads(hidden_grad, *side_saved(side))
        gate_grad = gate_grad.reshape(group_rows, half)
        up_grad = up_grad.reshape(group_rows, half)
        part_in = part_in + contract_last(gate_grad, w_half(side, 0))
        part_in = part_in + contract_last(up_grad, w_half(side, 1))
        for slot in range(2):
            columns = slice(slot * units, (slot + 1) * units)
            gate_part.append(contract_first(token_rows, gate_grad[:, columns]))
            up_part.append(contract_first(token_rows, up_grad[:, columns]))
    gate_wgrad, up_wgrad = (
        lax.psum_scatter(
            jnp.stack(parts).astype(jnp.bfloat16),
            "col",
            scatter_dimension=0,
            tiled=True,
            axis_index_groups=x_groups,
        )[0]
        for parts in (gate_part, up_part)
    )
    gate_wgrad = (gate_wgrad.astype(jnp.float32) * grad_scale).astype(jnp.bfloat16)
    up_wgrad = (up_wgrad.astype(jnp.float32) * grad_scale).astype(jnp.bfloat16)
    part_in, down_sum = lax.optimization_barrier((part_in, down_sum))
    down_wgrad = (down_sum.astype(jnp.float32) * grad_scale).astype(jnp.bfloat16)
    token_terms = exchange(
        part_in.astype(jnp.bfloat16).reshape(N_Z, block, features), "col", z_groups
    )
    token_grad = jnp.sum(token_terms.astype(jnp.float32), axis=0).astype(jnp.bfloat16)
    return (token_grad, gate_wgrad, up_wgrad, down_wgrad)


def solution(mesh):
    n_row, n_col = mesh.shape["row"], mesh.shape["col"]

    def device_program(*arrays):
        return local(n_row, n_col, *arrays)

    return jax.shard_map(
        device_program,
        mesh=mesh,
        in_specs=(
            P("col", "row"),
            P("col", "row"),
            P("row", "col"),
            P("row", "col"),
            P("row", "col"),
            P("row", "col"),
            P("col", "row"),
        ),
        out_specs=(P("col", "row"), P("row", "col"), P("row", "col"), P("col", "row")),
        check_vma=False,
    )
```

```python
import jax
import jax.numpy as jnp
from jax import lax
from jax.sharding import PartitionSpec as P

N_CORE = 2
N_Z = 8


def contract_last(left_side, right_side):
    return lax.dot_general(
        left_side, right_side, (((1,), (1,)), ((), ())), preferred_element_type=jnp.float32
    )


def contract_first(left_side, right_side):
    return lax.dot_general(
        left_side, right_side, (((0,), (0,)), ((), ())), preferred_element_type=jnp.float32
    )


def swiglu_grads(hidden_grad, gate_pre, up_pre):
    gate_float = gate_pre.astype(jnp.float32)
    up_float = up_pre.astype(jnp.float32)
    grad_float = hidden_grad.astype(jnp.float32)
    sigmoid_gate = jax.nn.sigmoid(gate_float)
    gate_grad = grad_float * up_float * sigmoid_gate * (1.0 + gate_float * (1.0 - sigmoid_gate))
    up_grad = grad_float * (gate_float * sigmoid_gate)
    return gate_grad.astype(jnp.bfloat16), up_grad.astype(jnp.bfloat16)


def swiglu_hidden(gate_pre, up_pre):
    gate_float = gate_pre.astype(jnp.float32)
    swish_gate = gate_float * jax.nn.sigmoid(gate_float)
    return (swish_gate * up_pre.astype(jnp.float32)).astype(jnp.bfloat16)


def exchange(pieces, axis, groups):
    return lax.all_to_all(pieces, axis, 0, 0, tiled=True, axis_index_groups=groups)


def spread(block, size, axis, groups):
    return exchange(jnp.broadcast_to(block[None], (size,) + block.shape), axis, groups)


def pick(stacked, index, axis=0):
    return lax.dynamic_index_in_dim(stacked, index, axis, keepdims=False)


def local(n_row, n_col, tokens, out_grad, gate_pre, up_pre, w_gate, w_up, w_down):
    n_y, n_x = n_row // N_CORE, n_col // N_Z
    z_groups = [[x * N_Z + z for z in range(N_Z)] for x in range(n_x)]
    x_groups = [[x * N_Z + z for x in range(n_x)] for z in range(N_Z)]
    y_groups = [[y * N_CORE + c for y in range(n_y)] for c in range(N_CORE)]
    core_swap = [(r, r ^ 1) for r in range(n_row)]
    row_here, col_here = lax.axis_index("row"), lax.axis_index("col")
    core, y_here = lax.rem(row_here, N_CORE), lax.div(row_here, N_CORE)
    x_here = lax.div(col_here, N_Z)
    rows, units = gate_pre.shape
    block, features = out_grad.shape
    half = 2 * units
    group_rows = N_Z * block

    def x_shift(step):
        return [
            (x * N_Z + z, (x + step) % n_x * N_Z + z) for x in range(n_x) for z in range(N_Z)
        ]

    def to_group(turn):
        pairs = []
        for r in range(n_row):
            for x in range(n_x):
                piece = (turn + x) % 2
                new_row = (2 * (r % n_x) + piece) * N_CORE + x // 2
                for z in range(N_Z):
                    pairs.append((r * n_col + x * N_Z + z, new_row * n_col + r // n_x * N_Z + z))
        return pairs

    down_stack = jnp.stack(
        [w_down] + [lax.ppermute(w_down, "col", x_shift(step)) for step in range(1, n_x)]
    )

    def down_half(side):
        first_block = 2 * lax.rem(core + side, 2)
        return jnp.concatenate(
            [
                pick(down_stack, lax.rem(x_here - first_block - slot + n_x, n_x))
                for slot in range(2)
            ]
        )

    grad_rows = spread(out_grad, N_Z, "col", z_groups).reshape(group_rows, features)

    saved_pieces = jnp.concatenate([gate_pre, up_pre], axis=1).reshape(2, block, half)
    moved = [
        lax.ppermute(
            pick(saved_pieces, lax.rem(x_here + turn, 2)), ("row", "col"), to_group(turn)
        )
        for turn in range(2)
    ]
    y_even = lax.rem(y_here, 2) == 0
    first = jnp.where(y_even, moved[0], moved[1])
    second = jnp.where(y_even, moved[1], moved[0])
    saved_share = jnp.concatenate(
        [first[:, :units], second[:, :units], first[:, units:], second[:, units:]], axis=1
    )
    saved = lax.all_gather(saved_share, "row", axis=0, tiled=True).reshape(
        n_y, N_CORE, block, 2 * half
    )

    both = jnp.concatenate([tokens, out_grad], axis=1)
    both, saved_share = lax.optimization_barrier((both, saved_share))
    token_rows = lax.all_gather(both, "col", axis=0, tiled=True, axis_index_groups=z_groups)[
        :, :features
    ]

    w_both = jnp.concatenate([w_gate, w_up], axis=1)
    w_both, grad_rows = lax.optimization_barrier((w_both, grad_rows))
    w_left = lax.ppermute(w_both, "col", x_shift(1))
    w_right = lax.ppermute(w_both, "col", x_shift(n_x - 1))
    w_far = lax.ppermute(w_left, "col", x_shift(1))

    give = contract_last(grad_rows, down_half(1)).astype(jnp.bfloat16)
    got = lax.ppermute(give, "row", core_swap)
    keep = contract_last(grad_rows, down_half(0)).astype(jnp.bfloat16)
    pair = (keep.astype(jnp.float32) + got.astype(jnp.float32)).astype(jnp.bfloat16)
    terms = exchange(pair.reshape(n_y, block, half), "row", y_groups)
    share = jnp.sum(terms.astype(jnp.float32), axis=0).astype(jnp.bfloat16)
    own = spread(share, n_y, "row", y_groups)

    grad_scale = (rows * n_row) ** (-0.5)

    def side_saved(side):
        return saved[:, side, :, :half], saved[:, side, :, half:]

    down_part = []
    for side in range(2):
        hidden = swiglu_hidden(*side_saved(side)).reshape(group_rows, half)
        down_part.append(contract_first(hidden, grad_rows).astype(jnp.bfloat16))
    down_part = jnp.concatenate(down_part, axis=0)
    own, _ = lax.optimization_barrier((own, down_part))
    down_sum = lax.psum_scatter(
        down_part,
        "col",
        scatter_dimension=0,
        tiled=True,
        axis_index_groups=x_groups,
    )

    own, w_left, w_right, w_far = lax.optimization_barrier((own, w_left, w_right, w_far))
    w_stack = jnp.stack([w_both, w_left, w_far, w_right])
    w_order = [pick(w_stack, lax.rem(x_here - place + n_x, n_x)) for place in range(n_x)]

    def w_half(side, which):
        pieces = w_order[2 * side : 2 * side + 2]
        return jnp.concatenate(
            [piece[:, which * units : (which + 1) * units] for piece in pieces], axis=1
        )

    other = lax.ppermute(own, "row", core_swap)
    part_in, gate_part, up_part = 0.0, [], []
    for side in range(2):
        hidden_grad = jnp.where(core == side, own, other)
        gate_grad, up_grad = swiglu_grads(hidden_grad, *side_saved(side))
        gate_grad = gate_grad.reshape(group_rows, half)
        up_grad = up_grad.reshape(group_rows, half)
        part_in = part_in + contract_last(gate_grad, w_half(side, 0))
        part_in = part_in + contract_last(up_grad, w_half(side, 1))
        for slot in range(2):
            columns = slice(slot * units, (slot + 1) * units)
            gate_part.append(contract_first(token_rows, gate_grad[:, columns]))
            up_part.append(contract_first(token_rows, up_grad[:, columns]))
    gate_sum = lax.psum_scatter(
        jnp.stack(gate_part).astype(jnp.bfloat16),
        "col",
        scatter_dimension=0,
        tiled=True,
        axis_index_groups=x_groups,
    )[0]
    gate_wgrad = (gate_sum.astype(jnp.float32) * grad_scale).astype(jnp.bfloat16)
    up_stack = jnp.stack(up_part)
    up_sum = pick(up_stack, x_here)
    for step in range(1, n_x):
        piece = pick(up_stack, lax.rem(x_here + step, n_x)).astype(jnp.bfloat16)
        up_sum = up_sum + lax.ppermute(piece, "col", x_shift(step)).astype(jnp.float32)
    up_wgrad = (up_sum * grad_scale).astype(jnp.bfloat16)
    part_in, down_sum = lax.optimization_barrier((part_in, down_sum))
    down_wgrad = (down_sum.astype(jnp.float32) * grad_scale).astype(jnp.bfloat16)
    token_terms = exchange(
        part_in.astype(jnp.bfloat16).reshape(N_Z, block, features), "col", z_groups
    )
    token_grad = jnp.sum(token_terms.astype(jnp.float32), axis=0).astype(jnp.bfloat16)
    return (token_grad, gate_wgrad, up_wgrad, down_wgrad)


def solution(mesh):
    n_row, n_col = mesh.shape["row"], mesh.shape["col"]

    def device_program(*arrays):
        return local(n_row, n_col, *arrays)

    return jax.shard_map(
        device_program,
        mesh=mesh,
        in_specs=(
            P("col", "row"),
            P("col", "row"),
            P("row", "col"),
            P("row", "col"),
            P("row", "col"),
            P("row", "col"),
            P("col", "row"),
        ),
        out_specs=(P("col", "row"), P("row", "col"), P("row", "col"), P("col", "row")),
        check_vma=False,
    )
```

```python
import jax
import jax.numpy as jnp
from jax import lax
from jax.experimental import pallas as pl
from jax.experimental.pallas import tpu as pltpu
from jax.sharding import PartitionSpec as P

N_CORE = 2
N_Z = 8


def contract_last(left_side, right_side):
    return lax.dot_general(
        left_side, right_side, (((1,), (1,)), ((), ())), preferred_element_type=jnp.float32
    )


def contract_first(left_side, right_side):
    return lax.dot_general(
        left_side, right_side, (((0,), (0,)), ((), ())), preferred_element_type=jnp.float32
    )


def swiglu_grads(hidden_grad, gate_pre, up_pre):
    gate_float = gate_pre.astype(jnp.float32)
    up_float = up_pre.astype(jnp.float32)
    grad_float = hidden_grad.astype(jnp.float32)
    sigmoid_gate = jax.nn.sigmoid(gate_float)
    gate_grad = grad_float * up_float * sigmoid_gate * (1.0 + gate_float * (1.0 - sigmoid_gate))
    up_grad = grad_float * (gate_float * sigmoid_gate)
    return gate_grad.astype(jnp.bfloat16), up_grad.astype(jnp.bfloat16)


def swiglu_hidden(gate_pre, up_pre):
    gate_float = gate_pre.astype(jnp.float32)
    swish_gate = gate_float * jax.nn.sigmoid(gate_float)
    return (swish_gate * up_pre.astype(jnp.float32)).astype(jnp.bfloat16)


def unit_block_kernel(
    place_ref, own_ref, other_ref, gate_ref, up_ref, tokens_ref,
    part_ref, gate_grad_ref, up_grad_ref, grad_ref,
):
    mine = pl.program_id(0) // 2 == place_ref[0]

    @pl.when(mine)
    def _():
        grad_ref[...] = own_ref[...].astype(jnp.float32)

    @pl.when(jnp.logical_not(mine))
    def _():
        grad_ref[...] = other_ref[...].astype(jnp.float32)

    shape = grad_ref.shape
    gate_grad, up_grad = swiglu_grads(
        grad_ref[...],
        gate_ref[...].astype(jnp.float32).reshape(shape),
        up_ref[...].astype(jnp.float32).reshape(shape),
    )
    gate_grad_ref[0] = gate_grad
    up_grad_ref[0] = up_grad
    token_columns = tokens_ref[...]
    units = shape[-1]
    for which, grads in enumerate((gate_grad, up_grad)):
        part_ref[0, :, which * units : (which + 1) * units] = jnp.dot(
            token_columns, grads, preferred_element_type=jnp.float32
        ).astype(jnp.bfloat16)


def unit_blocks(place, own, other, saved, token_columns):
    n_y, _, block, width = saved.shape
    units = width // 4
    features, group_rows = token_columns.shape
    n_block = 4

    def half_spec():
        return pl.BlockSpec((group_rows, units), lambda j, place: (0, j % 2))

    def saved_spec(first):
        return pl.BlockSpec(
            (n_y, 1, block, units), lambda j, place: (0, j // 2, 0, first + j % 2)
        )

    def out_spec(rows, width):
        return pl.BlockSpec((1, rows, width), lambda j, place: (j, 0, 0))

    part = jax.ShapeDtypeStruct((n_block, features, 2 * units), jnp.bfloat16)
    grads = jax.ShapeDtypeStruct((n_block, group_rows, units), jnp.bfloat16)
    return pl.pallas_call(
        unit_block_kernel,
        out_shape=(part, grads, grads),
        grid_spec=pltpu.PrefetchScalarGridSpec(
            num_scalar_prefetch=1,
            grid=(n_block,),
            in_specs=[
                half_spec(),
                half_spec(),
                saved_spec(0),
                saved_spec(2),
                pl.BlockSpec((features, group_rows), lambda j, place: (0, 0)),
            ],
            out_specs=[out_spec(features, 2 * units)] + [out_spec(group_rows, units)] * 2,
            scratch_shapes=[pltpu.VMEM((group_rows, units), jnp.float32)],
        ),
        compiler_params=pltpu.CompilerParams(vmem_limit_bytes=32 * 1024 * 1024),
        cost_estimate=pl.CostEstimate(
            flops=4 * n_block * features * units * group_rows,
            bytes_accessed=14_000_000,
            transcendentals=n_block * group_rows * units,
        ),
    )(place, own, other, saved, saved, token_columns)


def input_grad_kernel(order_ref, gate_ref, up_ref, *refs):
    weights, out_ref = refs[:-1], refs[-1]
    units = gate_ref.shape[-1]
    total = 0.0
    for step, weight_ref in enumerate(weights):
        place = order_ref[step]
        total = total + contract_last(gate_ref[place], weight_ref[:, :units])
        total = total + contract_last(up_ref[place], weight_ref[:, units:])
    out_ref[...] = total.astype(jnp.bfloat16)


def input_grad_part(order, gate_grad, up_grad, weights):
    n_block, group_rows, units = gate_grad.shape
    features = weights[0].shape[0]
    vmem = pl.BlockSpec(memory_space=pltpu.VMEM)
    return pl.pallas_call(
        input_grad_kernel,
        out_shape=jax.ShapeDtypeStruct((group_rows, features), jnp.bfloat16),
        in_specs=[pl.BlockSpec(memory_space=pltpu.SMEM)] + [vmem] * (2 + n_block),
        out_specs=vmem,
        compiler_params=pltpu.CompilerParams(vmem_limit_bytes=32 * 1024 * 1024),
        cost_estimate=pl.CostEstimate(
            flops=4 * n_block * features * units * group_rows,
            bytes_accessed=7_000_000,
            transcendentals=0,
        ),
    )(order, gate_grad, up_grad, *weights)


def exchange(pieces, axis, groups):
    return lax.all_to_all(pieces, axis, 0, 0, tiled=True, axis_index_groups=groups)


def spread(block, size, axis, groups):
    return exchange(jnp.broadcast_to(block[None], (size,) + block.shape), axis, groups)


def pick(stacked, index, axis=0):
    return lax.dynamic_index_in_dim(stacked, index, axis, keepdims=False)


def local(n_row, n_col, tokens, out_grad, gate_pre, up_pre, w_gate, w_up, w_down):
    n_y, n_x = n_row // N_CORE, n_col // N_Z
    z_groups = [[x * N_Z + z for z in range(N_Z)] for x in range(n_x)]
    x_groups = [[x * N_Z + z for x in range(n_x)] for z in range(N_Z)]
    y_groups = [[y * N_CORE + c for y in range(n_y)] for c in range(N_CORE)]
    core_swap = [(r, r ^ 1) for r in range(n_row)]
    row_here, col_here = lax.axis_index("row"), lax.axis_index("col")
    core, y_here = lax.rem(row_here, N_CORE), lax.div(row_here, N_CORE)
    x_here = lax.div(col_here, N_Z)
    rows, units = gate_pre.shape
    block, features = out_grad.shape
    half = 2 * units
    group_rows = N_Z * block

    def x_shift(step):
        return [
            (x * N_Z + z, (x + step) % n_x * N_Z + z) for x in range(n_x) for z in range(N_Z)
        ]

    def sum_over_x(parts):
        total = pick(parts, x_here).astype(jnp.float32)
        for step in range(1, n_x):
            piece = pick(parts, lax.rem(x_here + step, n_x))
            total = total + lax.ppermute(piece, "col", x_shift(step)).astype(jnp.float32)
        return total

    def to_group(turn):
        pairs = []
        for r in range(n_row):
            for x in range(n_x):
                piece = (turn + x) % 2
                new_row = (2 * (r % n_x) + piece) * N_CORE + x // 2
                for z in range(N_Z):
                    pairs.append((r * n_col + x * N_Z + z, new_row * n_col + r // n_x * N_Z + z))
        return pairs

    down_stack = jnp.stack(
        [w_down] + [lax.ppermute(w_down, "col", x_shift(step)) for step in range(1, n_x)]
    )

    def down_half(side):
        first_block = 2 * lax.rem(core + side, 2)
        return jnp.concatenate(
            [
                pick(down_stack, lax.rem(x_here - first_block - slot + n_x, n_x))
                for slot in range(2)
            ]
        )

    grad_rows = spread(out_grad, N_Z, "col", z_groups).reshape(group_rows, features)

    saved_pieces = jnp.concatenate([gate_pre, up_pre], axis=1).reshape(2, block, half)
    moved = [
        lax.ppermute(
            pick(saved_pieces, lax.rem(x_here + turn, 2)), ("row", "col"), to_group(turn)
        )
        for turn in range(2)
    ]
    y_even = lax.rem(y_here, 2) == 0
    first = jnp.where(y_even, moved[0], moved[1])
    second = jnp.where(y_even, moved[1], moved[0])
    saved_share = jnp.concatenate(
        [first[:, :units], second[:, :units], first[:, units:], second[:, units:]], axis=1
    )
    saved = lax.all_gather(saved_share, "row", axis=0, tiled=True).reshape(
        n_y, N_CORE, block, 2 * half
    )

    both = jnp.concatenate([tokens, out_grad], axis=1)
    both, saved_share = lax.optimization_barrier((both, saved_share))
    token_rows = lax.all_gather(both, "col", axis=0, tiled=True, axis_index_groups=z_groups)[
        :, :features
    ]

    w_both = jnp.concatenate([w_gate, w_up], axis=1)
    w_both, grad_rows = lax.optimization_barrier((w_both, grad_rows))
    w_left = lax.ppermute(w_both, "col", x_shift(1))
    w_right = lax.ppermute(w_both, "col", x_shift(n_x - 1))
    w_far = lax.ppermute(w_left, "col", x_shift(1))

    give = contract_last(grad_rows, down_half(1)).astype(jnp.bfloat16)
    got = lax.ppermute(give, "row", core_swap)
    keep = contract_last(grad_rows, down_half(0)).astype(jnp.bfloat16)
    pair = (keep.astype(jnp.float32) + got.astype(jnp.float32)).astype(jnp.bfloat16)
    terms = exchange(pair.reshape(n_y, block, half), "row", y_groups)
    share = jnp.sum(terms.astype(jnp.float32), axis=0).astype(jnp.bfloat16)
    own = spread(share, n_y, "row", y_groups).reshape(group_rows, half)

    grad_scale = (rows * n_row) ** (-0.5)

    def side_saved(side):
        return saved[:, side, :, :half], saved[:, side, :, half:]

    down_part = []
    for side in range(2):
        hidden = swiglu_hidden(*side_saved(side)).reshape(group_rows, half)
        down_part.append(contract_first(hidden, grad_rows).astype(jnp.bfloat16))
    down_part = jnp.concatenate(down_part, axis=0).reshape(n_x, units, features)
    own, _ = lax.optimization_barrier((own, down_part))
    down_sum = lax.psum_scatter(
        down_part, "col", scatter_dimension=0, tiled=True, axis_index_groups=x_groups
    )[0]

    own, w_left, w_right, w_far = lax.optimization_barrier((own, w_left, w_right, w_far))
    weights = [w_both, w_left, w_far, w_right]
    order = jnp.stack([lax.rem(x_here - step + n_x, n_x) for step in range(n_x)])

    other = lax.ppermute(own, "row", core_swap)
    unit_part, gate_grad, up_grad = unit_blocks(
        core.reshape(1), own, other, saved, token_rows.swapaxes(0, 1)
    )
    unit_wgrad = (sum_over_x(unit_part) * grad_scale).astype(jnp.bfloat16)
    gate_wgrad, up_wgrad = unit_wgrad[:, :units], unit_wgrad[:, units:]
    part_in = input_grad_part(order, gate_grad, up_grad, weights)
    part_in, down_sum = lax.optimization_barrier((part_in, down_sum))
    down_wgrad = (down_sum.astype(jnp.float32) * grad_scale).astype(jnp.bfloat16)
    token_terms = exchange(
        part_in.reshape(N_Z, block, features), "col", z_groups
    )
    token_grad = jnp.sum(token_terms.astype(jnp.float32), axis=0).astype(jnp.bfloat16)
    return (token_grad, gate_wgrad, up_wgrad, down_wgrad)


def solution(mesh):
    n_row, n_col = mesh.shape["row"], mesh.shape["col"]

    def device_program(*arrays):
        return local(n_row, n_col, *arrays)

    return jax.shard_map(
        device_program,
        mesh=mesh,
        in_specs=(
            P("col", "row"),
            P("col", "row"),
            P("row", "col"),
            P("row", "col"),
            P("row", "col"),
            P("row", "col"),
            P("col", "row"),
        ),
        out_specs=(P("col", "row"), P("row", "col"), P("row", "col"), P("col", "row")),
        check_vma=False,
    )
```

```python
import jax
import jax.numpy as jnp
from jax import lax
from jax.experimental import pallas as pl
from jax.experimental.pallas import tpu as pltpu
from jax.sharding import PartitionSpec as P

N_CORE = 2
N_Z = 8


def contract_last(left_side, right_side):
    return lax.dot_general(
        left_side, right_side, (((1,), (1,)), ((), ())), preferred_element_type=jnp.float32
    )


def contract_first(left_side, right_side):
    return lax.dot_general(
        left_side, right_side, (((0,), (0,)), ((), ())), preferred_element_type=jnp.float32
    )


def swiglu_grads(hidden_grad, gate_pre, up_pre):
    gate_float = gate_pre.astype(jnp.float32)
    up_float = up_pre.astype(jnp.float32)
    grad_float = hidden_grad.astype(jnp.float32)
    sigmoid_gate = jax.nn.sigmoid(gate_float)
    gate_grad = grad_float * up_float * sigmoid_gate * (1.0 + gate_float * (1.0 - sigmoid_gate))
    up_grad = grad_float * (gate_float * sigmoid_gate)
    return gate_grad.astype(jnp.bfloat16), up_grad.astype(jnp.bfloat16)


def swiglu_hidden(gate_pre, up_pre):
    gate_float = gate_pre.astype(jnp.float32)
    swish_gate = gate_float * jax.nn.sigmoid(gate_float)
    return (swish_gate * up_pre.astype(jnp.float32)).astype(jnp.bfloat16)


def unit_block_kernel(
    place_ref, own_ref, other_ref, gate_ref, up_ref, tokens_ref, *refs
):
    n_block = pl.num_programs(0)
    weights, parts = refs[:4], refs[4:8]
    input_part_ref, grad_ref, columns_ref, total_ref = refs[8:]
    step = pl.program_id(0)
    mine = lax.rem(place_ref[1] + step, n_block) // 2 == place_ref[0]

    @pl.when(step == 0)
    def _():
        columns_ref[...] = tokens_ref[...].T
        total_ref[...] = jnp.zeros_like(total_ref)

    @pl.when(mine)
    def _():
        grad_ref[...] = own_ref[...].astype(jnp.float32)

    @pl.when(jnp.logical_not(mine))
    def _():
        grad_ref[...] = other_ref[...].astype(jnp.float32)

    shape = grad_ref.shape
    units = shape[-1]
    gate_grad, up_grad = swiglu_grads(
        grad_ref[...],
        gate_ref[...].astype(jnp.float32).reshape(shape),
        up_ref[...].astype(jnp.float32).reshape(shape),
    )
    for k, part_ref in enumerate(parts):

        @pl.when(step == k)
        def _():
            weight_ref = weights[(len(parts) - k) % len(parts)]
            total = total_ref[...]
            for which, grads in enumerate((gate_grad, up_grad)):
                columns = slice(which * units, (which + 1) * units)
                part_ref[:, columns] = jnp.dot(
                    columns_ref[...], grads, preferred_element_type=jnp.float32
                ).astype(jnp.bfloat16)
                total = total + contract_last(grads, weight_ref[:, columns])
            total_ref[...] = total

    @pl.when(step == n_block - 1)
    def _():
        input_part_ref[...] = total_ref[...].astype(jnp.bfloat16)


def unit_blocks(place, own, other, saved, rows, weights):
    n_y, _, block, width = saved.shape
    units = width // 4
    group_rows = own.shape[0]
    features = weights[0].shape[0]
    n_block = len(weights)

    def block_of(j, place):
        return lax.rem(place[1] + j, n_block)

    def half_spec():
        return pl.BlockSpec(
            (group_rows, units), lambda j, place: (0, lax.rem(block_of(j, place), 2))
        )

    def saved_spec(first):
        def index(j, place):
            which = block_of(j, place)
            return (0, lax.div(which, 2), 0, first + lax.rem(which, 2))

        return pl.BlockSpec((n_y, 1, block, units), index)

    def fixed_spec(*shape):
        return pl.BlockSpec(shape, lambda j, place: (0, 0))

    part = jax.ShapeDtypeStruct((features, 2 * units), jnp.bfloat16)
    input_part = jax.ShapeDtypeStruct((group_rows, features), jnp.bfloat16)
    return pl.pallas_call(
        unit_block_kernel,
        out_shape=(part,) * n_block + (input_part,),
        grid_spec=pltpu.PrefetchScalarGridSpec(
            num_scalar_prefetch=1,
            grid=(n_block,),
            in_specs=[half_spec(), half_spec(), saved_spec(0), saved_spec(2)]
            + [fixed_spec(group_rows, features)]
            + [fixed_spec(features, 2 * units)] * n_block,
            out_specs=[fixed_spec(features, 2 * units)] * n_block
            + [fixed_spec(group_rows, features)],
            scratch_shapes=[
                pltpu.VMEM((group_rows, units), jnp.float32),
                pltpu.VMEM((features, group_rows), jnp.bfloat16),
                pltpu.VMEM((group_rows, features), jnp.float32),
            ],
        ),
        compiler_params=pltpu.CompilerParams(vmem_limit_bytes=40 * 1024 * 1024),
        cost_estimate=pl.CostEstimate(
            flops=8 * n_block * features * units * group_rows,
            bytes_accessed=14_000_000,
            transcendentals=n_block * group_rows * units,
        ),
    )(place, own, other, saved, saved, rows, *weights)


def exchange(pieces, axis, groups):
    return lax.all_to_all(pieces, axis, 0, 0, tiled=True, axis_index_groups=groups)


def spread(block, size, axis, groups):
    return exchange(jnp.broadcast_to(block[None], (size,) + block.shape), axis, groups)


def pick(stacked, index, axis=0):
    return lax.dynamic_index_in_dim(stacked, index, axis, keepdims=False)


def local(n_row, n_col, tokens, out_grad, gate_pre, up_pre, w_gate, w_up, w_down):
    n_y, n_x = n_row // N_CORE, n_col // N_Z
    z_groups = [[x * N_Z + z for z in range(N_Z)] for x in range(n_x)]
    x_groups = [[x * N_Z + z for x in range(n_x)] for z in range(N_Z)]
    y_groups = [[y * N_CORE + c for y in range(n_y)] for c in range(N_CORE)]
    core_swap = [(r, r ^ 1) for r in range(n_row)]
    row_here, col_here = lax.axis_index("row"), lax.axis_index("col")
    core, y_here = lax.rem(row_here, N_CORE), lax.div(row_here, N_CORE)
    x_here = lax.div(col_here, N_Z)
    rows, units = gate_pre.shape
    block, features = out_grad.shape
    half = 2 * units
    group_rows = N_Z * block

    def x_shift(step):
        return [
            (x * N_Z + z, (x + step) % n_x * N_Z + z) for x in range(n_x) for z in range(N_Z)
        ]

    def to_group(turn):
        pairs = []
        for r in range(n_row):
            for x in range(n_x):
                piece = (turn + x) % 2
                new_row = (2 * (r % n_x) + piece) * N_CORE + x // 2
                for z in range(N_Z):
                    pairs.append((r * n_col + x * N_Z + z, new_row * n_col + r // n_x * N_Z + z))
        return pairs

    down_stack = jnp.stack(
        [w_down] + [lax.ppermute(w_down, "col", x_shift(step)) for step in range(1, n_x)]
    )

    def down_half(side):
        first_block = 2 * lax.rem(core + side, 2)
        return jnp.concatenate(
            [
                pick(down_stack, lax.rem(x_here - first_block - slot + n_x, n_x))
                for slot in range(2)
            ]
        )

    grad_rows = spread(out_grad, N_Z, "col", z_groups).reshape(group_rows, features)

    saved_pieces = jnp.concatenate([gate_pre, up_pre], axis=1).reshape(2, block, half)
    moved = [
        lax.ppermute(
            pick(saved_pieces, lax.rem(x_here + turn, 2)), ("row", "col"), to_group(turn)
        )
        for turn in range(2)
    ]
    y_even = lax.rem(y_here, 2) == 0
    first = jnp.where(y_even, moved[0], moved[1])
    second = jnp.where(y_even, moved[1], moved[0])
    saved_share = jnp.concatenate(
        [first[:, :units], second[:, :units], first[:, units:], second[:, units:]], axis=1
    )
    saved = lax.all_gather(saved_share, "row", axis=0, tiled=True).reshape(
        n_y, N_CORE, block, 2 * half
    )

    both = jnp.concatenate([tokens, out_grad], axis=1)
    both, saved_share = lax.optimization_barrier((both, saved_share))
    both_rows = lax.all_gather(both, "col", axis=0, tiled=True, axis_index_groups=z_groups)

    w_both = jnp.concatenate([w_gate, w_up], axis=1)
    w_both, grad_rows = lax.optimization_barrier((w_both, grad_rows))
    w_left = lax.ppermute(w_both, "col", x_shift(1))
    w_right = lax.ppermute(w_both, "col", x_shift(n_x - 1))

    give = contract_last(grad_rows, down_half(1)).astype(jnp.bfloat16)
    got = lax.ppermute(give, "row", core_swap)
    keep = contract_last(grad_rows, down_half(0)).astype(jnp.bfloat16)
    pair = (keep.astype(jnp.float32) + got.astype(jnp.float32)).astype(jnp.bfloat16)
    terms = exchange(pair.reshape(n_y, block, half), "row", y_groups)
    share = jnp.sum(terms.astype(jnp.float32), axis=0).astype(jnp.bfloat16)
    share, w_left, w_right = lax.optimization_barrier((share, w_left, w_right))
    w_far = lax.ppermute(w_left, "col", x_shift(1))
    own = spread(share, n_y, "row", y_groups).reshape(group_rows, half)

    grad_scale = (rows * n_row) ** (-0.5)

    def side_saved(side):
        return saved[:, side, :, :half], saved[:, side, :, half:]

    down_part = []
    for side in range(2):
        hidden = swiglu_hidden(*side_saved(side)).reshape(group_rows, half)
        down_part.append(contract_first(hidden, grad_rows).astype(jnp.bfloat16))
    down_part = jnp.concatenate(down_part, axis=0).reshape(n_x, units, features)
    own, _ = lax.optimization_barrier((own, down_part))
    down_sum = lax.psum_scatter(
        down_part, "col", scatter_dimension=0, tiled=True, axis_index_groups=x_groups
    )[0]

    own, w_far = lax.optimization_barrier((own, w_far))
    weights = [w_both, w_left, w_far, w_right]

    other = lax.ppermute(own, "row", core_swap)
    *unit_parts, part_in = unit_blocks(
        jnp.stack([core, x_here]), own, other, saved, both_rows, weights
    )
    unit_sum = unit_parts[0].astype(jnp.float32)
    for step in range(1, n_x):
        moved_part = lax.ppermute(unit_parts[step], "col", x_shift(step))
        unit_sum = unit_sum + moved_part.astype(jnp.float32)
    unit_wgrad = (unit_sum * grad_scale).astype(jnp.bfloat16)
    gate_wgrad, up_wgrad = unit_wgrad[:, :units], unit_wgrad[:, units:]
    part_in, down_sum = lax.optimization_barrier((part_in, down_sum))
    down_wgrad = (down_sum.astype(jnp.float32) * grad_scale).astype(jnp.bfloat16)
    token_terms = exchange(
        part_in.reshape(N_Z, block, features), "col", z_groups
    )
    token_grad = jnp.sum(token_terms.astype(jnp.float32), axis=0).astype(jnp.bfloat16)
    return (token_grad, gate_wgrad, up_wgrad, down_wgrad)


def solution(mesh):
    n_row, n_col = mesh.shape["row"], mesh.shape["col"]

    def device_program(*arrays):
        return local(n_row, n_col, *arrays)

    return jax.shard_map(
        device_program,
        mesh=mesh,
        in_specs=(
            P("col", "row"),
            P("col", "row"),
            P("row", "col"),
            P("row", "col"),
            P("row", "col"),
            P("row", "col"),
            P("col", "row"),
        ),
        out_specs=(P("col", "row"), P("row", "col"), P("row", "col"), P("col", "row")),
        check_vma=False,
    )
```

```python
import jax
import jax.numpy as jnp
from jax import lax
from jax.experimental import pallas as pl
from jax.experimental.pallas import tpu as pltpu
from jax.sharding import PartitionSpec as P

N_CORE = 2
N_Z = 8


def contract_last(left_side, right_side):
    return lax.dot_general(
        left_side, right_side, (((1,), (1,)), ((), ())), preferred_element_type=jnp.float32
    )


def contract_first(left_side, right_side):
    return lax.dot_general(
        left_side, right_side, (((0,), (0,)), ((), ())), preferred_element_type=jnp.float32
    )


def swiglu_grads(hidden_grad, gate_pre, up_pre):
    gate_float = gate_pre.astype(jnp.float32)
    up_float = up_pre.astype(jnp.float32)
    grad_float = hidden_grad.astype(jnp.float32)
    sigmoid_gate = jax.nn.sigmoid(gate_float)
    gate_grad = grad_float * up_float * sigmoid_gate * (1.0 + gate_float * (1.0 - sigmoid_gate))
    up_grad = grad_float * (gate_float * sigmoid_gate)
    return gate_grad.astype(jnp.bfloat16), up_grad.astype(jnp.bfloat16)


def swiglu_hidden(gate_pre, up_pre):
    gate_float = gate_pre.astype(jnp.float32)
    swish_gate = gate_float * jax.nn.sigmoid(gate_float)
    return (swish_gate * up_pre.astype(jnp.float32)).astype(jnp.bfloat16)


def unit_block_kernel(place_ref, own_ref, other_ref, gate_ref, up_ref, tokens_ref, *refs):
    *parts, grads_ref, grad_ref, columns_ref = refs
    step = pl.program_id(0)
    mine = lax.rem(place_ref[1] + step, len(parts)) // 2 == place_ref[0]

    @pl.when(step == 0)
    def _():
        columns_ref[...] = tokens_ref[...].T

    @pl.when(mine)
    def _():
        grad_ref[...] = own_ref[...].astype(jnp.float32)

    @pl.when(jnp.logical_not(mine))
    def _():
        grad_ref[...] = other_ref[...].astype(jnp.float32)

    shape = grad_ref.shape
    units = shape[-1]
    gate_grad, up_grad = swiglu_grads(
        grad_ref[...],
        gate_ref[...].astype(jnp.float32).reshape(shape),
        up_ref[...].astype(jnp.float32).reshape(shape),
    )
    grads_ref[:, :units] = gate_grad
    grads_ref[:, units:] = up_grad
    for k, part_ref in enumerate(parts):

        @pl.when(step == k)
        def _():
            part_ref[...] = jnp.dot(
                columns_ref[...], grads_ref[...], preferred_element_type=jnp.float32
            ).astype(jnp.bfloat16)


def unit_blocks(place, own, other, saved, rows, n_block):
    n_y, _, block, width = saved.shape
    units = width // 4
    group_rows = own.shape[0]
    features = rows.shape[1] // 2

    def block_of(j, place):
        return lax.rem(place[1] + j, n_block)

    def half_spec():
        return pl.BlockSpec(
            (group_rows, units), lambda j, place: (0, lax.rem(block_of(j, place), 2))
        )

    def saved_spec(first):
        def index(j, place):
            which = block_of(j, place)
            return (0, lax.div(which, 2), 0, first + lax.rem(which, 2))

        return pl.BlockSpec((n_y, 1, block, units), index)

    def fixed_spec(*shape):
        return pl.BlockSpec(shape, lambda j, place: (0, 0))

    part = jax.ShapeDtypeStruct((features, 2 * units), jnp.bfloat16)
    grads = jax.ShapeDtypeStruct((group_rows, 2 * units * n_block), jnp.bfloat16)
    return pl.pallas_call(
        unit_block_kernel,
        out_shape=(part,) * n_block + (grads,),
        grid_spec=pltpu.PrefetchScalarGridSpec(
            num_scalar_prefetch=1,
            grid=(n_block,),
            in_specs=[half_spec(), half_spec(), saved_spec(0), saved_spec(2)]
            + [fixed_spec(group_rows, features)],
            out_specs=[fixed_spec(features, 2 * units)] * n_block
            + [pl.BlockSpec((group_rows, 2 * units), lambda j, place: (0, j))],
            scratch_shapes=[
                pltpu.VMEM((group_rows, units), jnp.float32),
                pltpu.VMEM((features, group_rows), jnp.bfloat16),
            ],
        ),
        compiler_params=pltpu.CompilerParams(vmem_limit_bytes=32 * 1024 * 1024),
        cost_estimate=pl.CostEstimate(
            flops=4 * n_block * features * units * group_rows,
            bytes_accessed=14_000_000,
            transcendentals=n_block * group_rows * units,
        ),
    )(place, own, other, saved, saved, rows)


def exchange(pieces, axis, groups):
    return lax.all_to_all(pieces, axis, 0, 0, tiled=True, axis_index_groups=groups)


def spread(block, size, axis, groups):
    return exchange(jnp.broadcast_to(block[None], (size,) + block.shape), axis, groups)


def pick(stacked, index, axis=0):
    return lax.dynamic_index_in_dim(stacked, index, axis, keepdims=False)


def local(n_row, n_col, tokens, out_grad, gate_pre, up_pre, w_gate, w_up, w_down):
    n_y, n_x = n_row // N_CORE, n_col // N_Z
    z_groups = [[x * N_Z + z for z in range(N_Z)] for x in range(n_x)]
    x_groups = [[x * N_Z + z for x in range(n_x)] for z in range(N_Z)]
    y_groups = [[y * N_CORE + c for y in range(n_y)] for c in range(N_CORE)]
    core_swap = [(r, r ^ 1) for r in range(n_row)]
    row_here, col_here = lax.axis_index("row"), lax.axis_index("col")
    core, y_here = lax.rem(row_here, N_CORE), lax.div(row_here, N_CORE)
    x_here = lax.div(col_here, N_Z)
    rows, units = gate_pre.shape
    block, features = out_grad.shape
    half = 2 * units
    group_rows = N_Z * block

    def x_shift(step):
        return [
            (x * N_Z + z, (x + step) % n_x * N_Z + z) for x in range(n_x) for z in range(N_Z)
        ]

    def to_group(turn):
        pairs = []
        for r in range(n_row):
            for x in range(n_x):
                piece = (turn + x) % 2
                new_row = (2 * (r % n_x) + piece) * N_CORE + x // 2
                for z in range(N_Z):
                    pairs.append((r * n_col + x * N_Z + z, new_row * n_col + r // n_x * N_Z + z))
        return pairs

    down_stack = jnp.stack(
        [w_down] + [lax.ppermute(w_down, "col", x_shift(step)) for step in range(1, n_x)]
    )

    def down_half(side):
        first_block = 2 * lax.rem(core + side, 2)
        return jnp.concatenate(
            [
                pick(down_stack, lax.rem(x_here - first_block - slot + n_x, n_x))
                for slot in range(2)
            ]
        )

    grad_rows = spread(out_grad, N_Z, "col", z_groups).reshape(group_rows, features)

    saved_pieces = jnp.concatenate([gate_pre, up_pre], axis=1).reshape(2, block, half)
    moved = [
        lax.ppermute(
            pick(saved_pieces, lax.rem(x_here + turn, 2)), ("row", "col"), to_group(turn)
        )
        for turn in range(2)
    ]
    y_even = lax.rem(y_here, 2) == 0
    first = jnp.where(y_even, moved[0], moved[1])
    second = jnp.where(y_even, moved[1], moved[0])
    saved_share = jnp.concatenate(
        [first[:, :units], second[:, :units], first[:, units:], second[:, units:]], axis=1
    )
    saved = lax.all_gather(saved_share, "row", axis=0, tiled=True).reshape(
        n_y, N_CORE, block, 2 * half
    )

    both = jnp.concatenate([tokens, out_grad], axis=1)
    both, saved_share = lax.optimization_barrier((both, saved_share))
    both_rows = lax.all_gather(both, "col", axis=0, tiled=True, axis_index_groups=z_groups)

    w_both = jnp.concatenate([w_gate, w_up], axis=1)
    w_both, grad_rows = lax.optimization_barrier((w_both, grad_rows))
    w_left = lax.ppermute(w_both, "col", x_shift(1))
    w_right = lax.ppermute(w_both, "col", x_shift(n_x - 1))

    give = contract_last(grad_rows, down_half(1)).astype(jnp.bfloat16)
    got = lax.ppermute(give, "row", core_swap)
    keep = contract_last(grad_rows, down_half(0)).astype(jnp.bfloat16)
    pair = (keep.astype(jnp.float32) + got.astype(jnp.float32)).astype(jnp.bfloat16)
    terms = exchange(pair.reshape(n_y, block, half), "row", y_groups)
    share = jnp.sum(terms.astype(jnp.float32), axis=0).astype(jnp.bfloat16)
    share, w_left, w_right = lax.optimization_barrier((share, w_left, w_right))
    w_far = lax.ppermute(w_left, "col", x_shift(1))
    own = spread(share, n_y, "row", y_groups).reshape(group_rows, half)

    grad_scale = (rows * n_row) ** (-0.5)

    def side_saved(side):
        return saved[:, side, :, :half], saved[:, side, :, half:]

    down_part = []
    for side in range(2):
        hidden = swiglu_hidden(*side_saved(side)).reshape(group_rows, half)
        down_part.append(contract_first(hidden, grad_rows).astype(jnp.bfloat16))
    down_part = jnp.concatenate(down_part, axis=0).reshape(n_x, units, features)
    down_part, w_far = lax.optimization_barrier((down_part, w_far))
    weights = jnp.concatenate([w_both, w_right, w_far, w_left], axis=1)
    down_sum = lax.psum_scatter(
        down_part, "col", scatter_dimension=0, tiled=True, axis_index_groups=x_groups
    )[0]
    own, weights, _ = lax.optimization_barrier((own, weights, down_part))

    other = lax.ppermute(own, "row", core_swap)
    *unit_parts, unit_grads = unit_blocks(
        jnp.stack([core, x_here]), own, other, saved, both_rows, n_x
    )
    part_in = contract_last(unit_grads, weights).astype(jnp.bfloat16)
    unit_sum = unit_parts[0].astype(jnp.float32)
    for step in range(1, n_x):
        moved_part = lax.ppermute(unit_parts[step], "col", x_shift(step))
        unit_sum = unit_sum + moved_part.astype(jnp.float32)
    unit_wgrad = (unit_sum * grad_scale).astype(jnp.bfloat16)
    gate_wgrad, up_wgrad = unit_wgrad[:, :units], unit_wgrad[:, units:]
    part_in, down_sum = lax.optimization_barrier((part_in, down_sum))
    down_wgrad = (down_sum.astype(jnp.float32) * grad_scale).astype(jnp.bfloat16)
    token_terms = exchange(
        part_in.reshape(N_Z, block, features), "col", z_groups
    )
    token_grad = jnp.sum(token_terms.astype(jnp.float32), axis=0).astype(jnp.bfloat16)
    return (token_grad, gate_wgrad, up_wgrad, down_wgrad)


def solution(mesh):
    n_row, n_col = mesh.shape["row"], mesh.shape["col"]

    def device_program(*arrays):
        return local(n_row, n_col, *arrays)

    return jax.shard_map(
        device_program,
        mesh=mesh,
        in_specs=(
            P("col", "row"),
            P("col", "row"),
            P("row", "col"),
            P("row", "col"),
            P("row", "col"),
            P("row", "col"),
            P("col", "row"),
        ),
        out_specs=(P("col", "row"), P("row", "col"), P("row", "col"), P("col", "row")),
        check_vma=False,
    )
```

```python
import jax
import jax.numpy as jnp
from jax import lax
from jax.experimental import pallas as pl
from jax.experimental.pallas import tpu as pltpu
from jax.sharding import PartitionSpec as P

N_CORE = 2
N_Z = 8


def contract_last(left_side, right_side):
    return lax.dot_general(
        left_side, right_side, (((1,), (1,)), ((), ())), preferred_element_type=jnp.float32
    )


def contract_first(left_side, right_side):
    return lax.dot_general(
        left_side, right_side, (((0,), (0,)), ((), ())), preferred_element_type=jnp.float32
    )


def swiglu_grads(hidden_grad, gate_pre, up_pre):
    gate_float = gate_pre.astype(jnp.float32)
    up_float = up_pre.astype(jnp.float32)
    grad_float = hidden_grad.astype(jnp.float32)
    sigmoid_gate = jax.nn.sigmoid(gate_float)
    gate_grad = grad_float * up_float * sigmoid_gate * (1.0 + gate_float * (1.0 - sigmoid_gate))
    up_grad = grad_float * (gate_float * sigmoid_gate)
    return gate_grad.astype(jnp.bfloat16), up_grad.astype(jnp.bfloat16)


def swiglu_hidden(gate_pre, up_pre):
    gate_float = gate_pre.astype(jnp.float32)
    swish_gate = gate_float * jax.nn.sigmoid(gate_float)
    return (swish_gate * up_pre.astype(jnp.float32)).astype(jnp.bfloat16)


def unit_block_kernel(place_ref, own_ref, other_ref, gate_ref, up_ref, tokens_ref, *refs):
    *parts, grads_ref, grad_ref = refs
    step = pl.program_id(0)
    mine = lax.rem(place_ref[1] + step, pl.num_programs(0)) // 2 == place_ref[0]

    @pl.when(mine)
    def _():
        grad_ref[...] = own_ref[...].astype(jnp.float32)

    @pl.when(jnp.logical_not(mine))
    def _():
        grad_ref[...] = other_ref[...].astype(jnp.float32)

    shape = grad_ref.shape
    units = shape[-1]
    gate_grad, up_grad = swiglu_grads(
        grad_ref[...],
        gate_ref[...].astype(jnp.float32).reshape(shape),
        up_ref[...].astype(jnp.float32).reshape(shape),
    )
    grads_ref[:, :units] = gate_grad
    grads_ref[:, units:] = up_grad
    for k, part_ref in enumerate(parts):

        @pl.when(step == k)
        def _():
            part_ref[...] = jnp.dot(
                tokens_ref[...], grads_ref[...], preferred_element_type=jnp.float32
            ).astype(jnp.bfloat16)


def unit_blocks(place, own, other, saved, token_columns, n_block):
    n_y, _, block, width = saved.shape
    units = width // 4
    group_rows = own.shape[0]
    features = token_columns.shape[0]

    def block_of(j, place):
        return lax.rem(place[1] + j, n_block)

    def half_spec():
        return pl.BlockSpec(
            (group_rows, units), lambda j, place: (0, lax.rem(block_of(j, place), 2))
        )

    def saved_spec(first):
        def index(j, place):
            which = block_of(j, place)
            return (0, lax.div(which, 2), 0, first + lax.rem(which, 2))

        return pl.BlockSpec((n_y, 1, block, units), index)

    def fixed_spec(*shape):
        return pl.BlockSpec(shape, lambda j, place: (0, 0))

    part = jax.ShapeDtypeStruct((features, 2 * units), jnp.bfloat16)
    grads = jax.ShapeDtypeStruct((group_rows, 2 * units * n_block), jnp.bfloat16)
    return pl.pallas_call(
        unit_block_kernel,
        out_shape=(part,) * n_block + (grads,),
        grid_spec=pltpu.PrefetchScalarGridSpec(
            num_scalar_prefetch=1,
            grid=(n_block,),
            in_specs=[half_spec(), half_spec(), saved_spec(0), saved_spec(2)]
            + [fixed_spec(features, group_rows)],
            out_specs=[fixed_spec(features, 2 * units)] * n_block
            + [pl.BlockSpec((group_rows, 2 * units), lambda j, place: (0, j))],
            scratch_shapes=[pltpu.VMEM((group_rows, units), jnp.float32)],
        ),
        compiler_params=pltpu.CompilerParams(vmem_limit_bytes=32 * 1024 * 1024),
        cost_estimate=pl.CostEstimate(
            flops=4 * n_block * features * units * group_rows,
            bytes_accessed=14_000_000,
            transcendentals=n_block * group_rows * units,
        ),
    )(place, own, other, saved, saved, token_columns)


def exchange(pieces, axis, groups):
    return lax.all_to_all(pieces, axis, 0, 0, tiled=True, axis_index_groups=groups)


def spread(block, size, axis, groups):
    return exchange(jnp.broadcast_to(block[None], (size,) + block.shape), axis, groups)


def pick(stacked, index, axis=0):
    return lax.dynamic_index_in_dim(stacked, index, axis, keepdims=False)


def local(n_row, n_col, tokens, out_grad, gate_pre, up_pre, w_gate, w_up, w_down):
    n_y, n_x = n_row // N_CORE, n_col // N_Z
    z_groups = [[x * N_Z + z for z in range(N_Z)] for x in range(n_x)]
    x_groups = [[x * N_Z + z for x in range(n_x)] for z in range(N_Z)]
    y_groups = [[y * N_CORE + c for y in range(n_y)] for c in range(N_CORE)]
    core_swap = [(r, r ^ 1) for r in range(n_row)]
    row_here, col_here = lax.axis_index("row"), lax.axis_index("col")
    core, y_here = lax.rem(row_here, N_CORE), lax.div(row_here, N_CORE)
    x_here = lax.div(col_here, N_Z)
    rows, units = gate_pre.shape
    block, features = out_grad.shape
    half = 2 * units
    group_rows = N_Z * block

    def x_shift(step):
        return [
            (x * N_Z + z, (x + step) % n_x * N_Z + z) for x in range(n_x) for z in range(N_Z)
        ]

    def to_group(turn):
        pairs = []
        for r in range(n_row):
            for x in range(n_x):
                piece = (turn + x) % 2
                new_row = (2 * (r % n_x) + piece) * N_CORE + x // 2
                for z in range(N_Z):
                    pairs.append((r * n_col + x * N_Z + z, new_row * n_col + r // n_x * N_Z + z))
        return pairs

    down_stack = jnp.stack(
        [w_down] + [lax.ppermute(w_down, "col", x_shift(step)) for step in range(1, n_x)]
    )

    def down_half(side):
        first_block = 2 * lax.rem(core + side, 2)
        return jnp.concatenate(
            [
                pick(down_stack, lax.rem(x_here - first_block - slot + n_x, n_x))
                for slot in range(2)
            ]
        )

    grad_rows = spread(out_grad, N_Z, "col", z_groups).reshape(group_rows, features)

    saved_pieces = jnp.concatenate([gate_pre, up_pre], axis=1).reshape(2, block, half)
    moved = [
        lax.ppermute(
            pick(saved_pieces, lax.rem(x_here + turn, 2)), ("row", "col"), to_group(turn)
        )
        for turn in range(2)
    ]
    y_even = lax.rem(y_here, 2) == 0
    first = jnp.where(y_even, moved[0], moved[1])
    second = jnp.where(y_even, moved[1], moved[0])
    saved_share = jnp.concatenate(
        [first[:, :units], second[:, :units], first[:, units:], second[:, units:]], axis=1
    )
    saved = lax.all_gather(saved_share, "row", axis=0, tiled=True).reshape(
        n_y, N_CORE, block, 2 * half
    )

    w_both = jnp.concatenate([w_gate, w_up], axis=1)
    w_both, grad_rows = lax.optimization_barrier((w_both, grad_rows))
    w_left = lax.ppermute(w_both, "col", x_shift(1))
    w_right = lax.ppermute(w_both, "col", x_shift(n_x - 1))

    give = contract_last(grad_rows, down_half(1)).astype(jnp.bfloat16)
    got = lax.ppermute(give, "row", core_swap)
    keep = contract_last(grad_rows, down_half(0)).astype(jnp.bfloat16)
    pair = (keep.astype(jnp.float32) + got.astype(jnp.float32)).astype(jnp.bfloat16)

    both = jnp.concatenate([tokens, out_grad], axis=1)
    both, pair = lax.optimization_barrier((both, pair))
    both_rows = lax.all_gather(both, "col", axis=0, tiled=True, axis_index_groups=z_groups)
    terms = exchange(pair.reshape(n_y, block, half), "row", y_groups)
    share = jnp.sum(terms.astype(jnp.float32), axis=0).astype(jnp.bfloat16)
    share, w_left, w_right = lax.optimization_barrier((share, w_left, w_right))
    w_far = lax.ppermute(w_left, "col", x_shift(1))
    own = spread(share, n_y, "row", y_groups).reshape(group_rows, half)

    grad_scale = (rows * n_row) ** (-0.5)

    def side_saved(side):
        return saved[:, side, :, :half], saved[:, side, :, half:]

    down_part = []
    for side in range(2):
        hidden = swiglu_hidden(*side_saved(side)).reshape(group_rows, half)
        down_part.append(contract_first(hidden, grad_rows).astype(jnp.bfloat16))
    down_part = jnp.concatenate(down_part, axis=0).reshape(n_x, units, features)
    down_part, w_far = lax.optimization_barrier((down_part, w_far))
    weights = [w_both, w_right, w_far, w_left]
    down_sum = lax.psum_scatter(
        down_part, "col", scatter_dimension=0, tiled=True, axis_index_groups=x_groups
    )[0]
    token_columns = both_rows[:, :features].swapaxes(0, 1)
    own, token_columns, _ = lax.optimization_barrier((own, token_columns, down_part))

    other = lax.ppermute(own, "row", core_swap)
    *unit_parts, unit_grads = unit_blocks(
        jnp.stack([core, x_here]), own, other, saved, token_columns, n_x
    )
    part_in = 0.0
    for step, weight in enumerate(weights):
        columns = slice(2 * step * units, 2 * (step + 1) * units)
        part_in = part_in + contract_last(unit_grads[:, columns], weight)
    part_in = part_in.astype(jnp.bfloat16)
    unit_sum = unit_parts[0].astype(jnp.float32)
    for step in range(1, n_x):
        moved_part = lax.ppermute(unit_parts[step], "col", x_shift(step))
        unit_sum = unit_sum + moved_part.astype(jnp.float32)
    unit_wgrad = (unit_sum * grad_scale).astype(jnp.bfloat16)
    gate_wgrad, up_wgrad = unit_wgrad[:, :units], unit_wgrad[:, units:]
    part_in, down_sum = lax.optimization_barrier((part_in, down_sum))
    down_wgrad = (down_sum.astype(jnp.float32) * grad_scale).astype(jnp.bfloat16)
    token_terms = exchange(
        part_in.reshape(N_Z, block, features), "col", z_groups
    )
    token_grad = jnp.sum(token_terms.astype(jnp.float32), axis=0).astype(jnp.bfloat16)
    return (token_grad, gate_wgrad, up_wgrad, down_wgrad)


def solution(mesh):
    n_row, n_col = mesh.shape["row"], mesh.shape["col"]

    def device_program(*arrays):
        return local(n_row, n_col, *arrays)

    return jax.shard_map(
        device_program,
        mesh=mesh,
        in_specs=(
            P("col", "row"),
            P("col", "row"),
            P("row", "col"),
            P("row", "col"),
            P("row", "col"),
            P("row", "col"),
            P("col", "row"),
        ),
        out_specs=(P("col", "row"), P("row", "col"), P("row", "col"), P("col", "row")),
        check_vma=False,
    )
```

```python
import jax
import jax.numpy as jnp
from jax import lax
from jax.experimental import pallas as pl
from jax.experimental.pallas import tpu as pltpu
from jax.sharding import PartitionSpec as P

N_CORE = 2
N_Z = 8


def contract_last(left_side, right_side):
    return lax.dot_general(
        left_side, right_side, (((1,), (1,)), ((), ())), preferred_element_type=jnp.float32
    )


def contract_first(left_side, right_side):
    return lax.dot_general(
        left_side, right_side, (((0,), (0,)), ((), ())), preferred_element_type=jnp.float32
    )


def swiglu_factors(gate_pre, up_pre):
    gate_float = gate_pre.astype(jnp.float32)
    up_float = up_pre.astype(jnp.float32)
    sigmoid_gate = jax.nn.sigmoid(gate_float)
    swish_gate = gate_float * sigmoid_gate
    gate_factor = up_float * sigmoid_gate * (1.0 + gate_float * (1.0 - sigmoid_gate))
    return (
        gate_factor.astype(jnp.bfloat16),
        swish_gate.astype(jnp.bfloat16),
        (swish_gate * up_float).astype(jnp.bfloat16),
    )


def unit_block_kernel(place_ref, own_ref, other_ref, gate_ref, up_ref, tokens_ref, *refs):
    *outs, grads_ref, parts_ref, columns_ref, sems = refs
    step, n_block = pl.program_id(0), pl.num_programs(0)
    mine = lax.rem(place_ref[1] + step, n_block) // 2 == place_ref[0]

    @pl.when(step == 0)
    def _():
        columns_ref[...] = tokens_ref[...].T

    hidden_grad = jnp.where(
        mine, own_ref[...].astype(jnp.float32), other_ref[...].astype(jnp.float32)
    )
    shape = hidden_grad.shape
    units = shape[-1]
    for which, factor_ref in enumerate((gate_ref, up_ref)):
        factor = factor_ref[...].astype(jnp.float32).reshape(shape)
        grads_ref[:, which * units : (which + 1) * units] = (hidden_grad * factor).astype(
            jnp.bfloat16
        )
    copies = [
        pltpu.make_async_copy(parts_ref.at[k], out_ref, sems.at[k])
        for k, out_ref in enumerate(outs)
    ]
    for k, copy in enumerate(copies):

        @pl.when(step == k)
        def _():
            parts_ref[k] = jnp.dot(
                columns_ref[...], grads_ref[...], preferred_element_type=jnp.float32
            ).astype(jnp.bfloat16)
            copy.start()

    @pl.when(step == n_block - 1)
    def _():
        for copy in copies:
            copy.wait()


def unit_blocks(place, own, other, gate_factor, up_factor, rows, n_block):
    n_y, _, block, half = gate_factor.shape
    units = half // 2
    group_rows = own.shape[0]
    features = rows.shape[1] // 2

    def block_of(j, place):
        return lax.rem(place[1] + j, n_block)

    def half_spec():
        return pl.BlockSpec(
            (group_rows, units), lambda j, place: (0, lax.rem(block_of(j, place), 2))
        )

    def factor_spec():
        def index(j, place):
            which = block_of(j, place)
            return (0, lax.div(which, 2), 0, lax.rem(which, 2))

        return pl.BlockSpec((n_y, 1, block, units), index)

    part = jax.ShapeDtypeStruct((features, 2 * units), jnp.bfloat16)
    grads = jax.ShapeDtypeStruct((group_rows, 2 * units * n_block), jnp.bfloat16)
    return pl.pallas_call(
        unit_block_kernel,
        out_shape=(part,) * n_block + (grads,),
        grid_spec=pltpu.PrefetchScalarGridSpec(
            num_scalar_prefetch=1,
            grid=(n_block,),
            in_specs=[half_spec(), half_spec(), factor_spec(), factor_spec()]
            + [pl.BlockSpec((group_rows, features), lambda j, place: (0, 0))],
            out_specs=[pl.BlockSpec(memory_space=pl.ANY)] * n_block
            + [pl.BlockSpec((group_rows, 2 * units), lambda j, place: (0, j))],
            scratch_shapes=[
                pltpu.VMEM((n_block, features, 2 * units), jnp.bfloat16),
                pltpu.VMEM((features, group_rows), jnp.bfloat16),
                pltpu.SemaphoreType.DMA((n_block,)),
            ],
        ),
        compiler_params=pltpu.CompilerParams(vmem_limit_bytes=32 * 1024 * 1024),
        cost_estimate=pl.CostEstimate(
            flops=4 * n_block * features * units * group_rows,
            bytes_accessed=14_000_000,
            transcendentals=0,
        ),
    )(place, own, other, gate_factor, up_factor, rows)


def exchange(pieces, axis, groups):
    return lax.all_to_all(pieces, axis, 0, 0, tiled=True, axis_index_groups=groups)


def spread(block, size, axis, groups):
    return exchange(jnp.broadcast_to(block[None], (size,) + block.shape), axis, groups)


def pick(stacked, index, axis=0):
    return lax.dynamic_index_in_dim(stacked, index, axis, keepdims=False)


def local(n_row, n_col, tokens, out_grad, gate_pre, up_pre, w_gate, w_up, w_down):
    n_y, n_x = n_row // N_CORE, n_col // N_Z
    z_groups = [[x * N_Z + z for z in range(N_Z)] for x in range(n_x)]
    x_groups = [[x * N_Z + z for x in range(n_x)] for z in range(N_Z)]
    y_groups = [[y * N_CORE + c for y in range(n_y)] for c in range(N_CORE)]
    core_swap = [(r, r ^ 1) for r in range(n_row)]
    row_here, col_here = lax.axis_index("row"), lax.axis_index("col")
    core, y_here = lax.rem(row_here, N_CORE), lax.div(row_here, N_CORE)
    x_here = lax.div(col_here, N_Z)
    rows, units = gate_pre.shape
    block, features = out_grad.shape
    half = 2 * units
    group_rows = N_Z * block

    def x_shift(step):
        return [
            (x * N_Z + z, (x + step) % n_x * N_Z + z) for x in range(n_x) for z in range(N_Z)
        ]

    def to_group(turn):
        pairs = []
        for r in range(n_row):
            for x in range(n_x):
                piece = (turn + x) % 2
                new_row = (2 * (r % n_x) + piece) * N_CORE + x // 2
                for z in range(N_Z):
                    pairs.append((r * n_col + x * N_Z + z, new_row * n_col + r // n_x * N_Z + z))
        return pairs

    down_stack = jnp.stack(
        [w_down] + [lax.ppermute(w_down, "col", x_shift(step)) for step in range(1, n_x)]
    )

    def down_half(side):
        first_block = 2 * lax.rem(core + side, 2)
        return jnp.concatenate(
            [
                pick(down_stack, lax.rem(x_here - first_block - slot + n_x, n_x))
                for slot in range(2)
            ]
        )

    grad_rows = spread(out_grad, N_Z, "col", z_groups).reshape(group_rows, features)

    saved_pieces = jnp.concatenate([gate_pre, up_pre], axis=1).reshape(2, block, half)
    moved = [
        lax.ppermute(
            pick(saved_pieces, lax.rem(x_here + turn, 2)), ("row", "col"), to_group(turn)
        )
        for turn in range(2)
    ]
    y_even = lax.rem(y_here, 2) == 0
    first = jnp.where(y_even, moved[0], moved[1])
    second = jnp.where(y_even, moved[1], moved[0])
    saved_share = jnp.concatenate(
        [first[:, :units], second[:, :units], first[:, units:], second[:, units:]], axis=1
    )
    saved = lax.all_gather(saved_share, "row", axis=0, tiled=True).reshape(
        n_y, N_CORE, block, 2 * half
    )

    w_both = jnp.concatenate([w_gate, w_up], axis=1)
    w_both, grad_rows = lax.optimization_barrier((w_both, grad_rows))
    w_left = lax.ppermute(w_both, "col", x_shift(1))
    w_right = lax.ppermute(w_both, "col", x_shift(n_x - 1))

    give = contract_last(grad_rows, down_half(1)).astype(jnp.bfloat16)
    got = lax.ppermute(give, "row", core_swap)
    keep = contract_last(grad_rows, down_half(0)).astype(jnp.bfloat16)
    pair = (keep.astype(jnp.float32) + got.astype(jnp.float32)).astype(jnp.bfloat16)

    both = jnp.concatenate([tokens, out_grad], axis=1)
    both, pair = lax.optimization_barrier((both, pair))
    both_rows = lax.all_gather(both, "col", axis=0, tiled=True, axis_index_groups=z_groups)
    terms = exchange(pair.reshape(n_y, block, half), "row", y_groups)
    share = jnp.sum(terms.astype(jnp.float32), axis=0).astype(jnp.bfloat16)
    share, w_left, w_right = lax.optimization_barrier((share, w_left, w_right))
    w_far = lax.ppermute(w_left, "col", x_shift(1))
    own = spread(share, n_y, "row", y_groups).reshape(group_rows, half)

    grad_scale = (rows * n_row) ** (-0.5)

    gate_factor, up_factor, hidden = swiglu_factors(saved[..., :half], saved[..., half:])
    down_part = [
        contract_first(hidden[:, side].reshape(group_rows, half), grad_rows).astype(jnp.bfloat16)
        for side in range(2)
    ]
    down_part = jnp.concatenate(down_part, axis=0).reshape(n_x, units, features)
    down_part, w_far = lax.optimization_barrier((down_part, w_far))
    weights = [w_both, w_right, w_far, w_left]
    down_sum = lax.psum_scatter(
        down_part, "col", scatter_dimension=0, tiled=True, axis_index_groups=x_groups
    )[0]
    own, gate_factor, up_factor, _ = lax.optimization_barrier(
        (own, gate_factor, up_factor, down_part)
    )

    other = lax.ppermute(own, "row", core_swap)
    *unit_parts, unit_grads = unit_blocks(
        jnp.stack([core, x_here]), own, other, gate_factor, up_factor, both_rows, n_x
    )
    part_in = 0.0
    for step, weight in enumerate(weights):
        columns = slice(2 * step * units, 2 * (step + 1) * units)
        part_in = part_in + contract_last(unit_grads[:, columns], weight)
    part_in = part_in.astype(jnp.bfloat16)
    unit_sum = unit_parts[0].astype(jnp.float32)
    for step in range(1, n_x):
        moved_part = lax.ppermute(unit_parts[step], "col", x_shift(step))
        unit_sum = unit_sum + moved_part.astype(jnp.float32)
    unit_wgrad = (unit_sum * grad_scale).astype(jnp.bfloat16)
    gate_wgrad, up_wgrad = unit_wgrad[:, :units], unit_wgrad[:, units:]
    part_in, down_sum = lax.optimization_barrier((part_in, down_sum))
    down_wgrad = (down_sum.astype(jnp.float32) * grad_scale).astype(jnp.bfloat16)
    token_terms = exchange(
        part_in.reshape(N_Z, block, features), "col", z_groups
    )
    token_grad = jnp.sum(token_terms.astype(jnp.float32), axis=0).astype(jnp.bfloat16)
    return (token_grad, gate_wgrad, up_wgrad, down_wgrad)


def solution(mesh):
    n_row, n_col = mesh.shape["row"], mesh.shape["col"]

    def device_program(*arrays):
        return local(n_row, n_col, *arrays)

    return jax.shard_map(
        device_program,
        mesh=mesh,
        in_specs=(
            P("col", "row"),
            P("col", "row"),
            P("row", "col"),
            P("row", "col"),
            P("row", "col"),
            P("row", "col"),
            P("col", "row"),
        ),
        out_specs=(P("col", "row"), P("row", "col"), P("row", "col"), P("col", "row")),
        check_vma=False,
    )
```

```python
import jax
import jax.numpy as jnp
from jax import lax
from jax.experimental import pallas as pl
from jax.experimental.pallas import tpu as pltpu
from jax.sharding import PartitionSpec as P

N_CORE = 2
N_Z = 8


def contract_last(left_side, right_side):
    return lax.dot_general(
        left_side, right_side, (((1,), (1,)), ((), ())), preferred_element_type=jnp.float32
    )


def contract_first(left_side, right_side):
    return lax.dot_general(
        left_side, right_side, (((0,), (0,)), ((), ())), preferred_element_type=jnp.float32
    )


def swiglu_factors(gate_pre, up_pre):
    gate_float = gate_pre.astype(jnp.float32)
    up_float = up_pre.astype(jnp.float32)
    sigmoid_gate = jax.nn.sigmoid(gate_float)
    swish_gate = gate_float * sigmoid_gate
    gate_factor = up_float * sigmoid_gate * (1.0 + gate_float * (1.0 - sigmoid_gate))
    return (
        gate_factor.astype(jnp.bfloat16),
        swish_gate.astype(jnp.bfloat16),
        (swish_gate * up_float).astype(jnp.bfloat16),
    )


def unit_block_kernel(place_ref, own_ref, other_ref, gate_ref, up_ref, tokens_ref, *refs):
    *outs, grads_ref, parts_ref, columns_ref, sems = refs
    step, n_block = pl.program_id(0), pl.num_programs(0)
    mine = lax.rem(place_ref[1] + step, n_block) // 2 == place_ref[0]

    @pl.when(step == 0)
    def _():
        columns_ref[...] = tokens_ref[...].T

    hidden_grad = jnp.where(
        mine, own_ref[...].astype(jnp.float32), other_ref[...].astype(jnp.float32)
    )
    shape = hidden_grad.shape
    units = shape[-1]
    for which, factor_ref in enumerate((gate_ref, up_ref)):
        factor = factor_ref[...].astype(jnp.float32).reshape(shape)
        grads_ref[:, which * units : (which + 1) * units] = (hidden_grad * factor).astype(
            jnp.bfloat16
        )
    copies = [
        pltpu.make_async_copy(parts_ref.at[k], out_ref, sems.at[k])
        for k, out_ref in enumerate(outs)
    ]
    for k, copy in enumerate(copies):

        @pl.when(step == k)
        def _():
            parts_ref[k] = jnp.dot(
                columns_ref[...], grads_ref[...], preferred_element_type=jnp.float32
            ).astype(jnp.bfloat16)
            copy.start()

    @pl.when(step == n_block - 1)
    def _():
        for copy in copies:
            copy.wait()


def unit_blocks(place, own, other, gate_factor, up_factor, rows, n_block):
    n_y, _, block, half = gate_factor.shape
    units = half // 2
    group_rows = own.shape[0]
    features = rows.shape[1] // 2

    def block_of(j, place):
        return lax.rem(place[1] + j, n_block)

    def half_spec():
        return pl.BlockSpec(
            (group_rows, units), lambda j, place: (0, lax.rem(block_of(j, place), 2))
        )

    def factor_spec():
        def index(j, place):
            which = block_of(j, place)
            return (0, lax.div(which, 2), 0, lax.rem(which, 2))

        return pl.BlockSpec((n_y, 1, block, units), index)

    part = jax.ShapeDtypeStruct((features, 2 * units), jnp.bfloat16)
    grads = jax.ShapeDtypeStruct((group_rows, 2 * units * n_block), jnp.bfloat16)
    return pl.pallas_call(
        unit_block_kernel,
        out_shape=(part,) * n_block + (grads,),
        grid_spec=pltpu.PrefetchScalarGridSpec(
            num_scalar_prefetch=1,
            grid=(n_block,),
            in_specs=[half_spec(), half_spec(), factor_spec(), factor_spec()]
            + [pl.BlockSpec((group_rows, features), lambda j, place: (0, 0))],
            out_specs=[pl.BlockSpec(memory_space=pl.ANY)] * n_block
            + [pl.BlockSpec((group_rows, 2 * units), lambda j, place: (0, j))],
            scratch_shapes=[
                pltpu.VMEM((n_block, features, 2 * units), jnp.bfloat16),
                pltpu.VMEM((features, group_rows), jnp.bfloat16),
                pltpu.SemaphoreType.DMA((n_block,)),
            ],
        ),
        compiler_params=pltpu.CompilerParams(vmem_limit_bytes=32 * 1024 * 1024),
        cost_estimate=pl.CostEstimate(
            flops=4 * n_block * features * units * group_rows,
            bytes_accessed=14_000_000,
            transcendentals=0,
        ),
    )(place, own, other, gate_factor, up_factor, rows)


def exchange(pieces, axis, groups):
    return lax.all_to_all(pieces, axis, 0, 0, tiled=True, axis_index_groups=groups)


def spread(block, size, axis, groups):
    return exchange(jnp.broadcast_to(block[None], (size,) + block.shape), axis, groups)


def pick(stacked, index, axis=0):
    return lax.dynamic_index_in_dim(stacked, index, axis, keepdims=False)


def local(n_row, n_col, tokens, out_grad, gate_pre, up_pre, w_gate, w_up, w_down):
    n_y, n_x = n_row // N_CORE, n_col // N_Z
    z_groups = [[x * N_Z + z for z in range(N_Z)] for x in range(n_x)]
    x_groups = [[x * N_Z + z for x in range(n_x)] for z in range(N_Z)]
    y_groups = [[y * N_CORE + c for y in range(n_y)] for c in range(N_CORE)]
    core_swap = [(r, r ^ 1) for r in range(n_row)]
    row_here, col_here = lax.axis_index("row"), lax.axis_index("col")
    core, y_here = lax.rem(row_here, N_CORE), lax.div(row_here, N_CORE)
    x_here = lax.div(col_here, N_Z)
    rows, units = gate_pre.shape
    block, features = out_grad.shape
    half = 2 * units
    group_rows = N_Z * block

    def x_shift(step):
        return [
            (x * N_Z + z, (x + step) % n_x * N_Z + z) for x in range(n_x) for z in range(N_Z)
        ]

    def to_group(turn):
        pairs = []
        for r in range(n_row):
            for x in range(n_x):
                piece = (turn + x) % 2
                new_row = (2 * (r % n_x) + piece) * N_CORE + x // 2
                for z in range(N_Z):
                    pairs.append((r * n_col + x * N_Z + z, new_row * n_col + r // n_x * N_Z + z))
        return pairs

    down_stack = jnp.stack(
        [w_down] + [lax.ppermute(w_down, "col", x_shift(step)) for step in range(1, n_x)]
    )

    def down_half(side):
        first_block = 2 * lax.rem(core + side, 2)
        return jnp.concatenate(
            [
                pick(down_stack, lax.rem(x_here - first_block - slot + n_x, n_x))
                for slot in range(2)
            ]
        )

    grad_rows = spread(out_grad, N_Z, "col", z_groups).reshape(group_rows, features)

    saved_pieces = jnp.concatenate([gate_pre, up_pre], axis=1).reshape(2, block, half)
    moved = [
        lax.ppermute(
            pick(saved_pieces, lax.rem(x_here + turn, 2)), ("row", "col"), to_group(turn)
        )
        for turn in range(2)
    ]
    y_even = lax.rem(y_here, 2) == 0
    first = jnp.where(y_even, moved[0], moved[1])
    second = jnp.where(y_even, moved[1], moved[0])
    saved_share = jnp.concatenate(
        [first[:, :units], second[:, :units], first[:, units:], second[:, units:]], axis=1
    )
    saved = lax.all_gather(saved_share, "row", axis=0, tiled=True).reshape(
        n_y, N_CORE, block, 2 * half
    )

    both = jnp.concatenate([tokens, out_grad], axis=1)
    both, saved_share = lax.optimization_barrier((both, saved_share))
    both_rows = lax.all_gather(both, "col", axis=0, tiled=True, axis_index_groups=z_groups)

    w_both = jnp.concatenate([w_gate, w_up], axis=1)
    w_both, grad_rows = lax.optimization_barrier((w_both, grad_rows))
    w_left = lax.ppermute(w_both, "col", x_shift(1))
    w_right = lax.ppermute(w_both, "col", x_shift(n_x - 1))

    give = contract_last(grad_rows, down_half(1)).astype(jnp.bfloat16)
    got = lax.ppermute(give, "row", core_swap)
    keep = contract_last(grad_rows, down_half(0)).astype(jnp.bfloat16)
    pair = (keep.astype(jnp.float32) + got.astype(jnp.float32)).astype(jnp.bfloat16)

    terms = exchange(pair.reshape(n_y, block, half), "row", y_groups)
    share = jnp.sum(terms.astype(jnp.float32), axis=0).astype(jnp.bfloat16)
    share, w_left, w_right = lax.optimization_barrier((share, w_left, w_right))
    w_far = lax.ppermute(w_left, "col", x_shift(1))
    own = spread(share, n_y, "row", y_groups).reshape(group_rows, half)

    grad_scale = (rows * n_row) ** (-0.5)

    gate_factor, up_factor, hidden = swiglu_factors(saved[..., :half], saved[..., half:])
    down_part = [
        contract_first(hidden[:, side].reshape(group_rows, half), grad_rows).astype(jnp.bfloat16)
        for side in range(2)
    ]
    down_part = jnp.concatenate(down_part, axis=0).reshape(n_x, units, features)
    down_sum = lax.psum_scatter(
        down_part, "col", scatter_dimension=0, tiled=True, axis_index_groups=x_groups
    )[0]
    own, gate_factor, up_factor, w_far, _ = lax.optimization_barrier(
        (own, gate_factor, up_factor, w_far, down_part)
    )
    weights = [w_both, w_right, w_far, w_left]

    other = lax.ppermute(own, "row", core_swap)
    *unit_parts, unit_grads = unit_blocks(
        jnp.stack([core, x_here]), own, other, gate_factor, up_factor, both_rows, n_x
    )
    unit_grads, down_sum = lax.optimization_barrier((unit_grads, down_sum))
    part_in = 0.0
    for step, weight in enumerate(weights):
        columns = slice(2 * step * units, 2 * (step + 1) * units)
        part_in = part_in + contract_last(unit_grads[:, columns], weight)
    part_in = part_in.astype(jnp.bfloat16)
    unit_sum = unit_parts[0].astype(jnp.float32)
    for step in range(1, n_x):
        moved_part = lax.ppermute(unit_parts[step], "col", x_shift(step))
        unit_sum = unit_sum + moved_part.astype(jnp.float32)
    unit_wgrad = (unit_sum * grad_scale).astype(jnp.bfloat16)
    gate_wgrad, up_wgrad = unit_wgrad[:, :units], unit_wgrad[:, units:]
    down_wgrad = (down_sum.astype(jnp.float32) * grad_scale).astype(jnp.bfloat16)
    token_terms = exchange(
        part_in.reshape(N_Z, block, features), "col", z_groups
    )
    token_grad = jnp.sum(token_terms.astype(jnp.float32), axis=0).astype(jnp.bfloat16)
    return (token_grad, gate_wgrad, up_wgrad, down_wgrad)


def solution(mesh):
    n_row, n_col = mesh.shape["row"], mesh.shape["col"]

    def device_program(*arrays):
        return local(n_row, n_col, *arrays)

    return jax.shard_map(
        device_program,
        mesh=mesh,
        in_specs=(
            P("col", "row"),
            P("col", "row"),
            P("row", "col"),
            P("row", "col"),
            P("row", "col"),
            P("row", "col"),
            P("col", "row"),
        ),
        out_specs=(P("col", "row"), P("row", "col"), P("row", "col"), P("col", "row")),
        check_vma=False,
    )
```

```python
import jax
import jax.numpy as jnp
from jax import lax
from jax.experimental import pallas as pl
from jax.experimental.pallas import tpu as pltpu
from jax.sharding import PartitionSpec as P

N_CORE = 2
N_Z = 8


def contract_last(left_side, right_side):
    return lax.dot_general(
        left_side, right_side, (((1,), (1,)), ((), ())), preferred_element_type=jnp.float32
    )


def contract_first(left_side, right_side):
    return lax.dot_general(
        left_side, right_side, (((0,), (0,)), ((), ())), preferred_element_type=jnp.float32
    )


def swiglu_factors(gate_pre, up_pre):
    gate_float = gate_pre.astype(jnp.float32)
    up_float = up_pre.astype(jnp.float32)
    sigmoid_gate = jax.nn.sigmoid(gate_float)
    swish_gate = gate_float * sigmoid_gate
    gate_factor = up_float * sigmoid_gate * (1.0 + gate_float * (1.0 - sigmoid_gate))
    return (
        gate_factor.astype(jnp.bfloat16),
        swish_gate.astype(jnp.bfloat16),
        (swish_gate * up_float).astype(jnp.bfloat16),
    )


def unit_block_kernel(place_ref, own_ref, other_ref, gate_ref, up_ref, tokens_ref, *refs):
    *outs, grads_ref, parts_ref, columns_ref, sems = refs
    step, n_block = pl.program_id(0), pl.num_programs(0)
    mine = lax.rem(place_ref[1] + step, n_block) // 2 == place_ref[0]

    @pl.when(step == 0)
    def _():
        columns_ref[...] = tokens_ref[...].T

    hidden_grad = jnp.where(
        mine, own_ref[...].astype(jnp.float32), other_ref[...].astype(jnp.float32)
    )
    shape = hidden_grad.shape
    units = shape[-1]
    for which, factor_ref in enumerate((gate_ref, up_ref)):
        factor = factor_ref[...].astype(jnp.float32).reshape(shape)
        grads_ref[:, which * units : (which + 1) * units] = (hidden_grad * factor).astype(
            jnp.bfloat16
        )
    copies = [
        pltpu.make_async_copy(parts_ref.at[k], out_ref, sems.at[k])
        for k, out_ref in enumerate(outs)
    ]
    for k, copy in enumerate(copies):

        @pl.when(step == k)
        def _():
            parts_ref[k] = jnp.dot(
                columns_ref[...], grads_ref[...], preferred_element_type=jnp.float32
            ).astype(jnp.bfloat16)
            copy.start()

    @pl.when(step == n_block - 1)
    def _():
        for copy in copies:
            copy.wait()


def unit_blocks(place, own, other, gate_factor, up_factor, rows, n_block):
    n_y, _, block, half = gate_factor.shape
    units = half // 2
    group_rows = own.shape[0]
    features = rows.shape[1] // 2

    def block_of(j, place):
        return lax.rem(place[1] + j, n_block)

    def half_spec():
        return pl.BlockSpec(
            (group_rows, units), lambda j, place: (0, lax.rem(block_of(j, place), 2))
        )

    def factor_spec():
        def index(j, place):
            which = block_of(j, place)
            return (0, lax.div(which, 2), 0, lax.rem(which, 2))

        return pl.BlockSpec((n_y, 1, block, units), index)

    part = jax.ShapeDtypeStruct((features, 2 * units), jnp.bfloat16)
    grads = jax.ShapeDtypeStruct((group_rows, 2 * units * n_block), jnp.bfloat16)
    return pl.pallas_call(
        unit_block_kernel,
        out_shape=(part,) * n_block + (grads,),
        grid_spec=pltpu.PrefetchScalarGridSpec(
            num_scalar_prefetch=1,
            grid=(n_block,),
            in_specs=[half_spec(), half_spec(), factor_spec(), factor_spec()]
            + [pl.BlockSpec((group_rows, features), lambda j, place: (0, 0))],
            out_specs=[pl.BlockSpec(memory_space=pl.ANY)] * n_block
            + [pl.BlockSpec((group_rows, 2 * units), lambda j, place: (0, j))],
            scratch_shapes=[
                pltpu.VMEM((n_block, features, 2 * units), jnp.bfloat16),
                pltpu.VMEM((features, group_rows), jnp.bfloat16),
                pltpu.SemaphoreType.DMA((n_block,)),
            ],
        ),
        compiler_params=pltpu.CompilerParams(vmem_limit_bytes=32 * 1024 * 1024),
        cost_estimate=pl.CostEstimate(
            flops=4 * n_block * features * units * group_rows,
            bytes_accessed=14_000_000,
            transcendentals=0,
        ),
    )(place, own, other, gate_factor, up_factor, rows)


def exchange(pieces, axis, groups):
    return lax.all_to_all(pieces, axis, 0, 0, tiled=True, axis_index_groups=groups)


def spread(block, size, axis, groups):
    return exchange(jnp.broadcast_to(block[None], (size,) + block.shape), axis, groups)


def pick(stacked, index, axis=0):
    return lax.dynamic_index_in_dim(stacked, index, axis, keepdims=False)


def local(n_row, n_col, tokens, out_grad, gate_pre, up_pre, w_gate, w_up, w_down):
    n_y, n_x = n_row // N_CORE, n_col // N_Z
    z_groups = [[x * N_Z + z for z in range(N_Z)] for x in range(n_x)]
    x_groups = [[x * N_Z + z for x in range(n_x)] for z in range(N_Z)]
    y_groups = [[y * N_CORE + c for y in range(n_y)] for c in range(N_CORE)]
    core_swap = [(r, r ^ 1) for r in range(n_row)]
    row_here, col_here = lax.axis_index("row"), lax.axis_index("col")
    core, y_here = lax.rem(row_here, N_CORE), lax.div(row_here, N_CORE)
    x_here = lax.div(col_here, N_Z)
    rows, units = gate_pre.shape
    block, features = out_grad.shape
    half = 2 * units
    group_rows = N_Z * block

    def x_shift(step):
        return [
            (x * N_Z + z, (x + step) % n_x * N_Z + z) for x in range(n_x) for z in range(N_Z)
        ]

    def to_group(turn):
        pairs = []
        for r in range(n_row):
            for x in range(n_x):
                piece = (turn + x) % 2
                new_row = (2 * (r % n_x) + piece) * N_CORE + x // 2
                for z in range(N_Z):
                    pairs.append((r * n_col + x * N_Z + z, new_row * n_col + r // n_x * N_Z + z))
        return pairs

    down_stack = jnp.stack(
        [w_down] + [lax.ppermute(w_down, "col", x_shift(step)) for step in range(1, n_x)]
    )

    def down_half(side):
        first_block = 2 * lax.rem(core + side, 2)
        return jnp.concatenate(
            [
                pick(down_stack, lax.rem(x_here - first_block - slot + n_x, n_x))
                for slot in range(2)
            ]
        )

    grad_rows = spread(out_grad, N_Z, "col", z_groups).reshape(group_rows, features)

    saved_pieces = jnp.concatenate([gate_pre, up_pre], axis=1).reshape(2, block, half)
    moved = [
        lax.ppermute(
            pick(saved_pieces, lax.rem(x_here + turn, 2)), ("row", "col"), to_group(turn)
        )
        for turn in range(2)
    ]
    y_even = lax.rem(y_here, 2) == 0
    first = jnp.where(y_even, moved[0], moved[1])
    second = jnp.where(y_even, moved[1], moved[0])
    saved_share = jnp.concatenate(
        [first[:, :units], second[:, :units], first[:, units:], second[:, units:]], axis=1
    )
    saved = lax.all_gather(saved_share, "row", axis=0, tiled=True).reshape(
        n_y, N_CORE, block, 2 * half
    )

    both = jnp.concatenate([tokens, out_grad], axis=1)
    both, _ = lax.optimization_barrier((both, grad_rows))
    both_rows = lax.all_gather(both, "col", axis=0, tiled=True, axis_index_groups=z_groups)

    w_both = jnp.concatenate([w_gate, w_up], axis=1)
    w_both, grad_rows = lax.optimization_barrier((w_both, grad_rows))
    w_left = lax.ppermute(w_both, "col", x_shift(1))
    w_right = lax.ppermute(w_both, "col", x_shift(n_x - 1))

    give = contract_last(grad_rows, down_half(1)).astype(jnp.bfloat16)
    got = lax.ppermute(give, "row", core_swap)
    keep = contract_last(grad_rows, down_half(0)).astype(jnp.bfloat16)
    pair = (keep.astype(jnp.float32) + got.astype(jnp.float32)).astype(jnp.bfloat16)

    terms = exchange(pair.reshape(n_y, block, half), "row", y_groups)
    share = jnp.sum(terms.astype(jnp.float32), axis=0).astype(jnp.bfloat16)
    share, w_left, w_right = lax.optimization_barrier((share, w_left, w_right))
    w_far = lax.ppermute(w_left, "col", x_shift(1))
    own = spread(share, n_y, "row", y_groups).reshape(group_rows, half)

    grad_scale = (rows * n_row) ** (-0.5)

    gate_factor, up_factor, hidden = swiglu_factors(saved[..., :half], saved[..., half:])
    down_part = [
        contract_first(hidden[:, side].reshape(group_rows, half), grad_rows).astype(jnp.bfloat16)
        for side in range(2)
    ]
    down_part = jnp.concatenate(down_part, axis=0).reshape(n_x, units, features)
    down_part, w_far = lax.optimization_barrier((down_part, w_far))
    weights = [w_both, w_right, w_far, w_left]
    down_sum = lax.psum_scatter(
        down_part, "col", scatter_dimension=0, tiled=True, axis_index_groups=x_groups
    )[0]
    own, gate_factor, up_factor, both_rows, _ = lax.optimization_barrier(
        (own, gate_factor, up_factor, both_rows, down_part)
    )

    other = lax.ppermute(own, "row", core_swap)
    *unit_parts, unit_grads = unit_blocks(
        jnp.stack([core, x_here]), own, other, gate_factor, up_factor, both_rows, n_x
    )
    part_in = 0.0
    for step, weight in enumerate(weights):
        columns = slice(2 * step * units, 2 * (step + 1) * units)
        part_in = part_in + contract_last(unit_grads[:, columns], weight)
    part_in = part_in.astype(jnp.bfloat16)
    unit_sum = unit_parts[0].astype(jnp.float32)
    for step in range(1, n_x):
        moved_part = lax.ppermute(unit_parts[step], "col", x_shift(step))
        unit_sum = unit_sum + moved_part.astype(jnp.float32)
    unit_wgrad = (unit_sum * grad_scale).astype(jnp.bfloat16)
    gate_wgrad, up_wgrad = unit_wgrad[:, :units], unit_wgrad[:, units:]
    down_wgrad = (down_sum.astype(jnp.float32) * grad_scale).astype(jnp.bfloat16)
    token_terms = exchange(
        part_in.reshape(N_Z, block, features), "col", z_groups
    )
    token_grad = jnp.sum(token_terms.astype(jnp.float32), axis=0).astype(jnp.bfloat16)
    return (token_grad, gate_wgrad, up_wgrad, down_wgrad)


def solution(mesh):
    n_row, n_col = mesh.shape["row"], mesh.shape["col"]

    def device_program(*arrays):
        return local(n_row, n_col, *arrays)

    return jax.shard_map(
        device_program,
        mesh=mesh,
        in_specs=(
            P("col", "row"),
            P("col", "row"),
            P("row", "col"),
            P("row", "col"),
            P("row", "col"),
            P("row", "col"),
            P("col", "row"),
        ),
        out_specs=(P("col", "row"), P("row", "col"), P("row", "col"), P("col", "row")),
        check_vma=False,
    )
```

```python
import jax
import jax.numpy as jnp
from jax import lax
from jax.experimental import pallas as pl
from jax.experimental.pallas import tpu as pltpu
from jax.sharding import PartitionSpec as P

N_CORE = 2
N_Z = 8


def contract_last(left_side, right_side):
    return lax.dot_general(
        left_side, right_side, (((1,), (1,)), ((), ())), preferred_element_type=jnp.float32
    )


def contract_first(left_side, right_side):
    return lax.dot_general(
        left_side, right_side, (((0,), (0,)), ((), ())), preferred_element_type=jnp.float32
    )


def swiglu_factors(gate_pre, up_pre):
    gate_float = gate_pre.astype(jnp.float32)
    up_float = up_pre.astype(jnp.float32)
    sigmoid_gate = jax.nn.sigmoid(gate_float)
    swish_gate = gate_float * sigmoid_gate
    gate_factor = up_float * sigmoid_gate * (1.0 + gate_float * (1.0 - sigmoid_gate))
    return (
        gate_factor.astype(jnp.bfloat16),
        swish_gate.astype(jnp.bfloat16),
        (swish_gate * up_float).astype(jnp.bfloat16),
    )


def unit_block_kernel(place_ref, own_ref, other_ref, gate_ref, up_ref, tokens_ref, *refs):
    *outs, grads_ref, parts_ref, columns_ref, sems = refs
    step, n_block = pl.program_id(0), pl.num_programs(0)
    mine = lax.rem(place_ref[1] + step, n_block) // 2 == place_ref[0]

    @pl.when(step == 0)
    def _():
        columns_ref[...] = tokens_ref[...].T

    hidden_grad = jnp.where(
        mine, own_ref[...].astype(jnp.float32), other_ref[...].astype(jnp.float32)
    )
    shape = hidden_grad.shape
    units = shape[-1]
    for which, factor_ref in enumerate((gate_ref, up_ref)):
        factor = factor_ref[...].astype(jnp.float32).reshape(shape)
        grads_ref[:, which * units : (which + 1) * units] = (hidden_grad * factor).astype(
            jnp.bfloat16
        )
    copies = [
        pltpu.make_async_copy(parts_ref.at[k], out_ref, sems.at[k])
        for k, out_ref in enumerate(outs)
    ]
    for k, copy in enumerate(copies):

        @pl.when(step == k)
        def _():
            parts_ref[k] = jnp.dot(
                columns_ref[...], grads_ref[...], preferred_element_type=jnp.float32
            ).astype(jnp.bfloat16)
            copy.start()

    @pl.when(step == n_block - 1)
    def _():
        for copy in copies:
            copy.wait()


def unit_blocks(place, own, other, gate_factor, up_factor, rows, n_block):
    n_y, _, block, half = gate_factor.shape
    units = half // 2
    group_rows = own.shape[0]
    features = rows.shape[1] // 2

    def block_of(j, place):
        return lax.rem(place[1] + j, n_block)

    def half_spec():
        return pl.BlockSpec(
            (group_rows, units), lambda j, place: (0, lax.rem(block_of(j, place), 2))
        )

    def factor_spec():
        def index(j, place):
            which = block_of(j, place)
            return (0, lax.div(which, 2), 0, lax.rem(which, 2))

        return pl.BlockSpec((n_y, 1, block, units), index)

    part = jax.ShapeDtypeStruct((features, 2 * units), jnp.bfloat16)
    grads = jax.ShapeDtypeStruct((group_rows, 2 * units * n_block), jnp.bfloat16)
    return pl.pallas_call(
        unit_block_kernel,
        out_shape=(part,) * n_block + (grads,),
        grid_spec=pltpu.PrefetchScalarGridSpec(
            num_scalar_prefetch=1,
            grid=(n_block,),
            in_specs=[half_spec(), half_spec(), factor_spec(), factor_spec()]
            + [pl.BlockSpec((group_rows, features), lambda j, place: (0, 0))],
            out_specs=[pl.BlockSpec(memory_space=pl.ANY)] * n_block
            + [pl.BlockSpec((group_rows, 2 * units), lambda j, place: (0, j))],
            scratch_shapes=[
                pltpu.VMEM((n_block, features, 2 * units), jnp.bfloat16),
                pltpu.VMEM((features, group_rows), jnp.bfloat16),
                pltpu.SemaphoreType.DMA((n_block,)),
            ],
        ),
        compiler_params=pltpu.CompilerParams(vmem_limit_bytes=32 * 1024 * 1024),
        cost_estimate=pl.CostEstimate(
            flops=4 * n_block * features * units * group_rows,
            bytes_accessed=14_000_000,
            transcendentals=0,
        ),
    )(place, own, other, gate_factor, up_factor, rows)


def exchange(pieces, axis, groups):
    return lax.all_to_all(pieces, axis, 0, 0, tiled=True, axis_index_groups=groups)


def spread(block, size, axis, groups):
    return exchange(jnp.broadcast_to(block[None], (size,) + block.shape), axis, groups)


def pick(stacked, index, axis=0):
    return lax.dynamic_index_in_dim(stacked, index, axis, keepdims=False)


def local(n_row, n_col, tokens, out_grad, gate_pre, up_pre, w_gate, w_up, w_down):
    n_y, n_x = n_row // N_CORE, n_col // N_Z
    z_groups = [[x * N_Z + z for z in range(N_Z)] for x in range(n_x)]
    x_groups = [[x * N_Z + z for x in range(n_x)] for z in range(N_Z)]
    y_groups = [[y * N_CORE + c for y in range(n_y)] for c in range(N_CORE)]
    core_swap = [(r, r ^ 1) for r in range(n_row)]
    row_here, col_here = lax.axis_index("row"), lax.axis_index("col")
    core, y_here = lax.rem(row_here, N_CORE), lax.div(row_here, N_CORE)
    x_here = lax.div(col_here, N_Z)
    rows, units = gate_pre.shape
    block, features = out_grad.shape
    half = 2 * units
    group_rows = N_Z * block

    def x_shift(step):
        return [
            (x * N_Z + z, (x + step) % n_x * N_Z + z) for x in range(n_x) for z in range(N_Z)
        ]

    def to_group(turn):
        pairs = []
        for r in range(n_row):
            for x in range(n_x):
                piece = (turn + x) % 2
                new_row = (2 * (r % n_x) + piece) * N_CORE + x // 2
                for z in range(N_Z):
                    pairs.append((r * n_col + x * N_Z + z, new_row * n_col + r // n_x * N_Z + z))
        return pairs

    down_stack = jnp.stack(
        [w_down] + [lax.ppermute(w_down, "col", x_shift(step)) for step in range(1, n_x)]
    )

    def down_half(side):
        first_block = 2 * lax.rem(core + side, 2)
        return jnp.concatenate(
            [
                pick(down_stack, lax.rem(x_here - first_block - slot + n_x, n_x))
                for slot in range(2)
            ]
        )

    grad_rows = spread(out_grad, N_Z, "col", z_groups).reshape(group_rows, features)

    saved_pieces = jnp.concatenate([gate_pre, up_pre], axis=1).reshape(2, block, half)
    moved = [
        lax.ppermute(
            pick(saved_pieces, lax.rem(x_here + turn, 2)), ("row", "col"), to_group(turn)
        )
        for turn in range(2)
    ]
    y_even = lax.rem(y_here, 2) == 0
    first = jnp.where(y_even, moved[0], moved[1])
    second = jnp.where(y_even, moved[1], moved[0])
    saved_share = jnp.concatenate(
        [first[:, :units], second[:, :units], first[:, units:], second[:, units:]], axis=1
    )
    saved = lax.all_gather(saved_share, "row", axis=0, tiled=True).reshape(
        n_y, N_CORE, block, 2 * half
    )

    both = jnp.concatenate([tokens, out_grad], axis=1)
    both, saved_share = lax.optimization_barrier((both, saved_share))
    both_rows = lax.all_gather(both, "col", axis=0, tiled=True, axis_index_groups=z_groups)

    w_both = jnp.concatenate([w_gate, w_up], axis=1)
    w_both, grad_rows = lax.optimization_barrier((w_both, grad_rows))
    w_left = lax.ppermute(w_both, "col", x_shift(1))
    w_right = lax.ppermute(w_both, "col", x_shift(n_x - 1))

    give = contract_last(grad_rows, down_half(1)).astype(jnp.bfloat16)
    got = lax.ppermute(give, "row", core_swap)
    keep = contract_last(grad_rows, down_half(0)).astype(jnp.bfloat16)
    pair = (keep.astype(jnp.float32) + got.astype(jnp.float32)).astype(jnp.bfloat16)

    terms = exchange(pair.reshape(n_y, block, half), "row", y_groups)
    share = jnp.sum(terms.astype(jnp.float32), axis=0).astype(jnp.bfloat16)
    share, w_left, w_right = lax.optimization_barrier((share, w_left, w_right))
    w_far = jnp.concatenate(
        [
            lax.ppermute(w_left[: features // 2], "col", x_shift(1)),
            lax.ppermute(w_right[features // 2 :], "col", x_shift(n_x - 1)),
        ]
    )
    own = spread(share, n_y, "row", y_groups).reshape(group_rows, half)

    grad_scale = (rows * n_row) ** (-0.5)

    gate_factor, up_factor, hidden = swiglu_factors(saved[..., :half], saved[..., half:])
    down_part = [
        contract_first(hidden[:, side].reshape(group_rows, half), grad_rows).astype(jnp.bfloat16)
        for side in range(2)
    ]
    down_part = jnp.concatenate(down_part, axis=0).reshape(n_x, units, features)
    down_sum = lax.psum_scatter(
        down_part, "col", scatter_dimension=0, tiled=True, axis_index_groups=x_groups
    )[0]
    own, gate_factor, up_factor, w_left, w_right, w_far, _ = lax.optimization_barrier(
        (own, gate_factor, up_factor, w_left, w_right, w_far, down_part)
    )
    weights = [w_both, w_right, w_far, w_left]

    other = lax.ppermute(own, "row", core_swap)
    *unit_parts, unit_grads = unit_blocks(
        jnp.stack([core, x_here]), own, other, gate_factor, up_factor, both_rows, n_x
    )
    part_in = 0.0
    for step, weight in enumerate(weights):
        columns = slice(2 * step * units, 2 * (step + 1) * units)
        part_in = part_in + contract_last(unit_grads[:, columns], weight)
    part_in = part_in.astype(jnp.bfloat16)
    unit_sum = unit_parts[0].astype(jnp.float32)
    for step in range(1, n_x):
        moved_part = lax.ppermute(unit_parts[step], "col", x_shift(step))
        unit_sum = unit_sum + moved_part.astype(jnp.float32)
    unit_wgrad = (unit_sum * grad_scale).astype(jnp.bfloat16)
    gate_wgrad, up_wgrad = unit_wgrad[:, :units], unit_wgrad[:, units:]
    part_in, down_sum = lax.optimization_barrier((part_in, down_sum))
    down_wgrad = (down_sum.astype(jnp.float32) * grad_scale).astype(jnp.bfloat16)
    token_terms = exchange(
        part_in.reshape(N_Z, block, features), "col", z_groups
    )
    token_grad = jnp.sum(token_terms.astype(jnp.float32), axis=0).astype(jnp.bfloat16)
    return (token_grad, gate_wgrad, up_wgrad, down_wgrad)


def solution(mesh):
    n_row, n_col = mesh.shape["row"], mesh.shape["col"]

    def device_program(*arrays):
        return local(n_row, n_col, *arrays)

    return jax.shard_map(
        device_program,
        mesh=mesh,
        in_specs=(
            P("col", "row"),
            P("col", "row"),
            P("row", "col"),
            P("row", "col"),
            P("row", "col"),
            P("row", "col"),
            P("col", "row"),
        ),
        out_specs=(P("col", "row"), P("row", "col"), P("row", "col"), P("col", "row")),
        check_vma=False,
    )
```

```python
import jax
import jax.numpy as jnp
from jax import lax
from jax.experimental import pallas as pl
from jax.experimental.pallas import tpu as pltpu
from jax.sharding import PartitionSpec as P

N_CORE = 2
N_Z = 8


def contract_last(left_side, right_side):
    return lax.dot_general(
        left_side, right_side, (((1,), (1,)), ((), ())), preferred_element_type=jnp.float32
    )


def contract_first(left_side, right_side):
    return lax.dot_general(
        left_side, right_side, (((0,), (0,)), ((), ())), preferred_element_type=jnp.float32
    )


def swiglu_factors(gate_pre, up_pre):
    gate_float = gate_pre.astype(jnp.float32)
    up_float = up_pre.astype(jnp.float32)
    sigmoid_gate = jax.nn.sigmoid(gate_float)
    swish_gate = gate_float * sigmoid_gate
    gate_factor = up_float * sigmoid_gate * (1.0 + gate_float * (1.0 - sigmoid_gate))
    return (
        gate_factor.astype(jnp.bfloat16),
        swish_gate.astype(jnp.bfloat16),
        (swish_gate * up_float).astype(jnp.bfloat16),
    )


def unit_block_kernel(place_ref, own_ref, other_ref, gate_ref, up_ref, tokens_ref, *refs):
    *outs, grads_ref, parts_ref, columns_ref, sems = refs
    step, n_block = pl.program_id(0), pl.num_programs(0)
    mine = lax.rem(place_ref[1] + step, n_block) // 2 == place_ref[0]

    @pl.when(step == 0)
    def _():
        columns_ref[...] = tokens_ref[...].T

    hidden_grad = jnp.where(
        mine, own_ref[...].astype(jnp.float32), other_ref[...].astype(jnp.float32)
    )
    shape = hidden_grad.shape
    units = shape[-1]
    for which, factor_ref in enumerate((gate_ref, up_ref)):
        factor = factor_ref[...].astype(jnp.float32).reshape(shape)
        grads_ref[:, which * units : (which + 1) * units] = (hidden_grad * factor).astype(
            jnp.bfloat16
        )
    copies = [
        pltpu.make_async_copy(parts_ref.at[k], out_ref, sems.at[k])
        for k, out_ref in enumerate(outs)
    ]
    for k, copy in enumerate(copies):

        @pl.when(step == k)
        def _():
            parts_ref[k] = jnp.dot(
                columns_ref[...], grads_ref[...], preferred_element_type=jnp.float32
            ).astype(jnp.bfloat16)
            copy.start()

    @pl.when(step == n_block - 1)
    def _():
        for copy in copies:
            copy.wait()


def unit_blocks(place, own, other, gate_factor, up_factor, rows, n_block):
    n_y, _, block, half = gate_factor.shape
    units = half // 2
    group_rows = own.shape[0]
    features = rows.shape[1] // 2

    def block_of(j, place):
        return lax.rem(place[1] + j, n_block)

    def half_spec():
        return pl.BlockSpec(
            (group_rows, units), lambda j, place: (0, lax.rem(block_of(j, place), 2))
        )

    def factor_spec():
        def index(j, place):
            which = block_of(j, place)
            return (0, lax.div(which, 2), 0, lax.rem(which, 2))

        return pl.BlockSpec((n_y, 1, block, units), index)

    part = jax.ShapeDtypeStruct((features, 2 * units), jnp.bfloat16)
    grads = jax.ShapeDtypeStruct((group_rows, 2 * units * n_block), jnp.bfloat16)
    return pl.pallas_call(
        unit_block_kernel,
        out_shape=(part,) * n_block + (grads,),
        grid_spec=pltpu.PrefetchScalarGridSpec(
            num_scalar_prefetch=1,
            grid=(n_block,),
            in_specs=[half_spec(), half_spec(), factor_spec(), factor_spec()]
            + [pl.BlockSpec((group_rows, features), lambda j, place: (0, 0))],
            out_specs=[pl.BlockSpec(memory_space=pl.ANY)] * n_block
            + [pl.BlockSpec((group_rows, 2 * units), lambda j, place: (0, j))],
            scratch_shapes=[
                pltpu.VMEM((n_block, features, 2 * units), jnp.bfloat16),
                pltpu.VMEM((features, group_rows), jnp.bfloat16),
                pltpu.SemaphoreType.DMA((n_block,)),
            ],
        ),
        compiler_params=pltpu.CompilerParams(vmem_limit_bytes=32 * 1024 * 1024),
        cost_estimate=pl.CostEstimate(
            flops=4 * n_block * features * units * group_rows,
            bytes_accessed=14_000_000,
            transcendentals=0,
        ),
    )(place, own, other, gate_factor, up_factor, rows)


def exchange(pieces, axis, groups):
    return lax.all_to_all(pieces, axis, 0, 0, tiled=True, axis_index_groups=groups)


def spread(block, size, axis, groups):
    return exchange(jnp.broadcast_to(block[None], (size,) + block.shape), axis, groups)


def pick(stacked, index, axis=0):
    return lax.dynamic_index_in_dim(stacked, index, axis, keepdims=False)


def local(n_row, n_col, tokens, out_grad, gate_pre, up_pre, w_gate, w_up, w_down):
    n_y, n_x = n_row // N_CORE, n_col // N_Z
    z_groups = [[x * N_Z + z for z in range(N_Z)] for x in range(n_x)]
    x_groups = [[x * N_Z + z for x in range(n_x)] for z in range(N_Z)]
    y_groups = [[y * N_CORE + c for y in range(n_y)] for c in range(N_CORE)]
    core_swap = [(r, r ^ 1) for r in range(n_row)]
    row_here, col_here = lax.axis_index("row"), lax.axis_index("col")
    core, y_here = lax.rem(row_here, N_CORE), lax.div(row_here, N_CORE)
    x_here = lax.div(col_here, N_Z)
    rows, units = gate_pre.shape
    block, features = out_grad.shape
    half = 2 * units
    group_rows = N_Z * block

    def x_shift(step):
        return [
            (x * N_Z + z, (x + step) % n_x * N_Z + z) for x in range(n_x) for z in range(N_Z)
        ]

    def to_group(turn):
        pairs = []
        for r in range(n_row):
            for x in range(n_x):
                piece = (turn + x) % 2
                new_row = (2 * (r % n_x) + piece) * N_CORE + x // 2
                for z in range(N_Z):
                    pairs.append((r * n_col + x * N_Z + z, new_row * n_col + r // n_x * N_Z + z))
        return pairs

    down_stack = jnp.stack(
        [w_down] + [lax.ppermute(w_down, "col", x_shift(step)) for step in range(1, n_x)]
    )

    def down_half(side):
        first_block = 2 * lax.rem(core + side, 2)
        return jnp.concatenate(
            [
                pick(down_stack, lax.rem(x_here - first_block - slot + n_x, n_x))
                for slot in range(2)
            ]
        )

    grad_rows = spread(out_grad, N_Z, "col", z_groups).reshape(group_rows, features)

    saved_pieces = jnp.concatenate([gate_pre, up_pre], axis=1).reshape(2, block, half)
    moved = [
        lax.ppermute(
            pick(saved_pieces, lax.rem(x_here + turn, 2)), ("row", "col"), to_group(turn)
        )
        for turn in range(2)
    ]
    y_even = lax.rem(y_here, 2) == 0
    first = jnp.where(y_even, moved[0], moved[1])
    second = jnp.where(y_even, moved[1], moved[0])
    saved_share = jnp.concatenate(
        [first[:, :units], second[:, :units], first[:, units:], second[:, units:]], axis=1
    )
    saved = lax.all_gather(saved_share, "row", axis=0, tiled=True).reshape(
        n_y, N_CORE, block, 2 * half
    )

    both = jnp.concatenate([tokens, out_grad], axis=1)
    both, saved_share = lax.optimization_barrier((both, saved_share))
    both_rows = lax.all_gather(both, "col", axis=0, tiled=True, axis_index_groups=z_groups)

    w_both = jnp.concatenate([w_gate, w_up], axis=1)
    w_both, grad_rows = lax.optimization_barrier((w_both, grad_rows))
    w_left = lax.ppermute(w_both, "col", x_shift(1))
    w_right = lax.ppermute(w_both, "col", x_shift(n_x - 1))

    give = contract_last(grad_rows, down_half(1)).astype(jnp.bfloat16)
    got = lax.ppermute(give, "row", core_swap)
    keep = contract_last(grad_rows, down_half(0)).astype(jnp.bfloat16)
    pair = (keep.astype(jnp.float32) + got.astype(jnp.float32)).astype(jnp.bfloat16)

    terms = exchange(pair.reshape(n_y, block, half), "row", y_groups)
    share = jnp.sum(terms.astype(jnp.float32), axis=0).astype(jnp.bfloat16)
    share, w_left, w_right = lax.optimization_barrier((share, w_left, w_right))
    far_first = lax.ppermute(w_left[: features // 2], "col", x_shift(1))
    far_second = lax.ppermute(w_right[features // 2 :], "col", x_shift(n_x - 1))
    own = spread(share, n_y, "row", y_groups).reshape(group_rows, half)

    grad_scale = (rows * n_row) ** (-0.5)

    gate_factor, up_factor, hidden = swiglu_factors(saved[..., :half], saved[..., half:])
    down_part = [
        contract_first(hidden[:, side].reshape(group_rows, half), grad_rows).astype(jnp.bfloat16)
        for side in range(2)
    ]
    down_part = jnp.concatenate(down_part, axis=0).reshape(n_x, units, features)
    down_sum = lax.psum_scatter(
        down_part, "col", scatter_dimension=0, tiled=True, axis_index_groups=x_groups
    )[0]
    own, gate_factor, up_factor, w_left, w_right, far_first, far_second, _ = (
        lax.optimization_barrier(
            (own, gate_factor, up_factor, w_left, w_right, far_first, far_second, down_part)
        )
    )
    w_far = jnp.concatenate([far_first, far_second])
    weights = [w_both, w_right, w_far, w_left]

    other = lax.ppermute(own, "row", core_swap)
    *unit_parts, unit_grads = unit_blocks(
        jnp.stack([core, x_here]), own, other, gate_factor, up_factor, both_rows, n_x
    )
    part_in = 0.0
    for step, weight in enumerate(weights):
        columns = slice(2 * step * units, 2 * (step + 1) * units)
        part_in = part_in + contract_last(unit_grads[:, columns], weight)
    part_in = part_in.astype(jnp.bfloat16)
    unit_sum = unit_parts[0].astype(jnp.float32)
    for step in range(1, n_x):
        moved_part = lax.ppermute(unit_parts[step], "col", x_shift(step))
        unit_sum = unit_sum + moved_part.astype(jnp.float32)
    unit_wgrad = (unit_sum * grad_scale).astype(jnp.bfloat16)
    gate_wgrad, up_wgrad = unit_wgrad[:, :units], unit_wgrad[:, units:]
    part_in, down_sum = lax.optimization_barrier((part_in, down_sum))
    down_wgrad = (down_sum.astype(jnp.float32) * grad_scale).astype(jnp.bfloat16)
    token_terms = exchange(
        part_in.reshape(N_Z, block, features), "col", z_groups
    )
    token_grad = jnp.sum(token_terms.astype(jnp.float32), axis=0).astype(jnp.bfloat16)
    return (token_grad, gate_wgrad, up_wgrad, down_wgrad)


def solution(mesh):
    n_row, n_col = mesh.shape["row"], mesh.shape["col"]

    def device_program(*arrays):
        return local(n_row, n_col, *arrays)

    return jax.shard_map(
        device_program,
        mesh=mesh,
        in_specs=(
            P("col", "row"),
            P("col", "row"),
            P("row", "col"),
            P("row", "col"),
            P("row", "col"),
            P("row", "col"),
            P("col", "row"),
        ),
        out_specs=(P("col", "row"), P("row", "col"), P("row", "col"), P("col", "row")),
        check_vma=False,
    )
```
